256 devices in a mesh: seq: 32 (over y, z), head: 8 (over x, core).
Axes of the slice: x: 4, y: 4, z: 8, core: 2. Of those that a mesh axis runs over, the one named last changes fastest.
Arguments:
- queries: bfloat16 [4096, 4096], P('seq', 'head'), may hold values from -6 to 6
- keys: bfloat16 [4096, 4096], P('seq', 'head'), may hold values from -6 to 6
- values: bfloat16 [4096, 4096], P('seq', 'head'), may hold values from -6 to 6
- log_decay: float32 [32, 4096], P('head', 'seq'), may hold values from -1 to 0, as said below
- beta: float32 [32, 4096], P('head', 'seq'), may hold values from 0.001 to 0.6
- level_weights: float32 [10, 32, 4096], P(None, 'head', 'seq'), may hold values from 0.25 to 2
- document_ends: int32 [64], P('seq'), may hold values 0 or 1
- out_weight: bfloat16 [4096, 4096], P('head', 'seq'), may hold values from -0.09375 to 0.09375
- grad_y: bfloat16 [4096, 4096], P('seq', 'head'), may hold values from -6 to 6
- final_state_grad: float32 [32, 128, 128], P('head'), may hold values from -6 to 6
Outputs:
- layer_out: bfloat16 [4096, 4096], P('seq', 'head')
- grad_queries: bfloat16 [4096, 4096], P('seq', 'head')
- grad_values: bfloat16 [4096, 4096], P('seq', 'head')
The draws below stay inside these ranges and needn't reach their ends.
Inputs may be any that keep to these rules, and one draw needn't show every extreme that they name: `log_decay`: strictly negative.
All inputs are finite; a program needn't handle non-finite values. No bound on the sum of `document_ends` on one device may be relied on, other than what follows from the above.
Results may differ from the reference program's by a relative error of at most 0.023.
Values may be sent and summed in bfloat16 or wider, within the bound.
No kernel may reach another device: no remote copies, remote signals or barrier semaphores. Data moves between devices by JAX's collectives and lax.ppermute only.
A program may use at most 64 MiB of HBM per device.

```python
import math
import jax
import jax.numpy as jnp
from jax import lax

D = 4096
HEADS = 32
DK = 128
BLOCK = 64
LEVELS = 10
STREAM_POSITIONS = 4096
BLOCKS = 64
N_HEAD = 8


def draw_keys(key, part):
    key = jax.random.fold_in(key, 11)
    base_key, jitter_key = jax.random.split(key, 2)
    spread_factor = 0.6
    common_part = jax.random.normal(base_key, (BLOCKS, 1, HEADS, DK), jnp.float32)
    jitter_part = jax.random.normal(jitter_key, (BLOCKS, BLOCK, HEADS, DK), jnp.float32)
    combined = common_part + spread_factor * jitter_part
    return jnp.clip(combined, -6.0, 6.0).reshape(STREAM_POSITIONS, HEADS * DK).astype(jnp.bfloat16)


def draw_log_decay(key, part):
    first, second, final_segment, fourth = jax.random.split(key, 4)
    log_rate = jax.random.uniform(first, (HEADS, 1), jnp.float32, math.log(1.0 / STREAM_POSITIONS), math.log(1.0 / 30.0))
    jitter_noise = jax.random.uniform(second, (HEADS, STREAM_POSITIONS), jnp.float32, 0.5, 1.5)
    reference_entry = -jnp.exp(log_rate) * jitter_noise
    spike_magnitude = jax.random.randint(final_segment, (1, STREAM_POSITIONS), 0, max(STREAM_POSITIONS // 4, 2)) == 0
    decline_magnitude = jax.random.uniform(fourth, (HEADS, STREAM_POSITIONS), jnp.float32, 0.5, 0.8)
    return reference_entry + jnp.where(spike_magnitude, jnp.log(decline_magnitude), 0.0)


def draw_beta(key, part):
    key = jax.random.fold_in(key, 7)
    gentle_key, jitter_key, strong_key, choose_key = jax.random.split(key, 4)
    gentle_scale = jnp.exp(jax.random.uniform(gentle_key, (HEADS, 1), jnp.float32, math.log(0.003), math.log(0.2)))
    strong_scale = jax.random.uniform(strong_key, (HEADS, 1), jnp.float32, 0.25, 0.4)
    ordering = jax.random.permutation(choose_key, HEADS)
    heavy_heads = (ordering < max(HEADS // 4, 1))[:, None]
    head_scale = jnp.where(heavy_heads, strong_scale, gentle_scale)
    jitter_noise = jax.random.uniform(jitter_key, (HEADS, STREAM_POSITIONS), jnp.float32, 0.5, 1.5)
    return head_scale * jitter_noise


def place_ends(values, rng, least, top_value):
    longest = values.shape.index(max(values.shape))
    spots = []
    for shift in (0, 1):
        where = [jax.random.randint(jax.random.fold_in(rng, axis), (), 0, length) for axis, length in enumerate(values.shape)]
        where[longest] = (where[longest] + shift) % values.shape[longest]
        spots.append(tuple(where))
    return values.at[spots[0]].set(least).at[spots[1]].set(top_value)


def block_levels(own_key, extent, cuts, smallest, high):
    loudness = 1.0
    for position, blocks in cuts:
        steps = jax.random.uniform(jax.random.fold_in(jax.random.fold_in(own_key, 6), position), (blocks,), jnp.float32, smallest / len(cuts), high / len(cuts))
        loudness = loudness * jnp.repeat(jnp.exp(steps), extent[position] // blocks).reshape((-1,) + (1,) * (len(extent) - 1 - position))
    return loudness


def noise(own_key, dims, scale, bound, pieces=(), kind=jnp.bfloat16):
    entries = jax.random.normal(own_key, dims, jnp.float32) * scale
    if len(pieces) > 0:
        entries = block_levels(own_key, dims, pieces, -0.22, 0.18) * entries
    return jnp.clip(entries, min=-bound, max=bound).astype(kind)


def setup_inputs(seed: int = 0) -> dict:
    key_list = jax.random.split(jax.random.key(seed), 11)
    queries = noise(key_list[0], (STREAM_POSITIONS, HEADS * DK), 1.0, 6.0, ((0, 32), (1, 8)))
    keys = draw_keys(jax.random.fold_in(key_list[10], 71), 0)
    values = noise(key_list[2], (STREAM_POSITIONS, HEADS * DK), 1.0, 6.0, ((0, 32), (1, 8)))
    log_decay = draw_log_decay(jax.random.fold_in(key_list[10], 71), 0)
    beta = draw_beta(jax.random.fold_in(key_list[10], 71), 0)
    level_weights = jnp.clip(jnp.exp(math.log(2.0) - 2.0794415 * jax.random.uniform(key_list[5], (LEVELS, HEADS, STREAM_POSITIONS), jnp.float32) ** block_levels(key_list[5], (LEVELS, HEADS, STREAM_POSITIONS), ((1, 8), (2, 32)), -0.2, 0.2)), 0.25, 2.0)
    document_ends = place_ends((jax.random.randint(key_list[6], (BLOCKS,), 0, 16) < 1).astype(jnp.int32), jax.random.fold_in(key_list[6], 1), 0, 1)
    out_weight = noise(key_list[7], (HEADS * DK, D), (HEADS * DK) ** -0.5, 0.09375, ((0, 8), (1, 32)))
    grad_y = noise(key_list[8], (STREAM_POSITIONS, D), 1.0, 6.0, ((0, 32), (1, 8)))
    final_state_grad = noise(key_list[9], (HEADS, DK, DK), 1.0, 6.0, ((0, 8),), jnp.float32)
    return {"queries": queries, "keys": keys, "values": values, "log_decay": log_decay, "beta": beta, "level_weights": level_weights, "document_ends": document_ends, "out_weight": out_weight, "grad_y": grad_y, "final_state_grad": final_state_grad}


def exact_dot(form, first, second):
    return jnp.einsum(form, first, second, precision=lax.Precision.HIGHEST)

def unit_rows(matrix):
    return matrix * lax.rsqrt(lax.optimization_barrier(jnp.sum(matrix * matrix, -1, keepdims=True)) + 1e-06)

def block_core(query_raw, value_raw, key_unit, log_gate, write_rate):
    query_unit = unit_rows(query_raw)
    cumulative = jnp.cumsum(log_gate, -1)
    length = log_gate.shape[-1]
    key_size = key_unit.shape[-1]
    row_ids = lax.broadcasted_iota(jnp.int32, (length, length), 0)
    col_ids = lax.broadcasted_iota(jnp.int32, (length, length), 1)
    causal = row_ids >= col_ids
    strict = row_ids > col_ids
    spread = cumulative[..., :, None] - cumulative[..., None, :]
    decay = jnp.where(causal, jnp.exp(jnp.where(causal, spread, 0.0)), 0.0)
    key_gram = exact_dot('...td,...jd->...tj', key_unit, key_unit)
    lower = jnp.where(strict, write_rate[..., :, None] * decay * key_gram, 0.0)
    system = lower + jnp.eye(length, dtype=jnp.float32)
    right_hand = jnp.concatenate([(write_rate * jnp.exp(cumulative))[..., None] * key_unit, write_rate[..., None] * value_raw], -1)
    solved = jax.scipy.linalg.solve_triangular(system, right_hand, lower=True, unit_diagonal=True)
    weights_w = solved[..., :key_size]
    update_u = solved[..., key_size:]
    key_tail = jnp.exp(cumulative[..., -1:] - cumulative)[..., None] * key_unit
    ident = jnp.eye(key_size, dtype=jnp.float32)
    transition = jnp.exp(cumulative[..., -1])[..., None, None] * ident - exact_dot('...td,...te->...de', key_tail, weights_w)
    written = exact_dot('...td,...te->...de', key_tail, update_u)
    scores = decay * exact_dot('...td,...jd->...tj', query_unit, key_unit)
    query_eff = jnp.exp(cumulative)[..., None] * query_unit - exact_dot('...tj,...jd->...td', scores, weights_w)
    local_out = exact_dot('...tj,...je->...te', scores, update_u)
    return ((written, query_eff, local_out), transition)

def fenwick_forward(trans, writes, query_eff, grad_out, weight_list, bit_count):
    head_count, block_count, key_size = (trans.shape[0], trans.shape[1], trans.shape[2])
    value_size = writes.shape[-1]
    length = query_eff.shape[2]
    prefix_map = jnp.broadcast_to(jnp.eye(key_size, dtype=jnp.float32), trans.shape)
    range_trans, range_state = (trans, writes)
    out_extra = jnp.zeros(query_eff.shape[:3] + (value_size,), jnp.float32)
    grad_extra = jnp.zeros(query_eff.shape, jnp.float32)
    saved = []
    for level in range(bit_count):
        width = 2 ** level
        halves = block_count // (2 * width)
        low_trans = range_trans[:, 0::2]
        upper_transition = range_trans[:, 1::2]
        low_state = range_state[:, 0::2]
        upper_state = range_state[:, 1::2]
        paired = prefix_map.reshape(head_count, halves, 2, width, key_size, key_size)
        upper_map = paired[:, :, 1]
        query_up = query_eff.reshape(head_count, halves, 2, width, length, key_size)[:, :, 1]
        grad_up = grad_out.reshape(head_count, halves, 2, width, length, value_size)[:, :, 1]
        weight_up = weight_list[level].reshape(head_count, halves, 2, width, length)[:, :, 1][..., None]
        states = exact_dot('hmsij,hmjk->hmsik', upper_map, low_state)
        weighted = weight_up * grad_up
        out_up = weight_up * exact_dot('hmstd,hmsde->hmste', query_up, states)
        dquery_up = exact_dot('hmste,hmsde->hmstd', weighted, states)
        state_grads = exact_dot('hmstd,hmste->hmsde', query_up, weighted)
        out_extra = out_extra + jnp.stack([jnp.zeros_like(out_up), out_up], 2).reshape(out_extra.shape)
        grad_extra = grad_extra + jnp.stack([jnp.zeros_like(dquery_up), dquery_up], 2).reshape(grad_extra.shape)
        moved = exact_dot('hmsij,hmjk->hmsik', upper_map, low_trans)
        prefix_map = jnp.stack([paired[:, :, 0], moved], 2).reshape(prefix_map.shape)
        range_state = exact_dot('hmij,hmjk->hmik', upper_transition, low_state) + upper_state
        range_trans = exact_dot('hmij,hmjk->hmik', upper_transition, low_trans)
        saved.append((upper_transition, upper_map, state_grads))
    return (prefix_map, range_trans, range_state, out_extra, grad_extra, saved)

def fenwick_backward(top_grad, saved):
    range_grad = top_grad
    for level in reversed(range(len(saved))):
        upper_transition, upper_map, state_grads = saved[level]
        low_grad = exact_dot('hmji,hmjk->hmik', upper_transition, range_grad) + exact_dot('hmsji,hmsjk->hmik', upper_map, state_grads)
        shape = range_grad.shape
        range_grad = jnp.stack([low_grad, range_grad], 2).reshape(shape[0], 2 * shape[1], shape[2], shape[3])
    return range_grad

def one_head(query_head, key_head, payload_channel, gate_head, rate_head, weight_head, head_gradient, final_head, keep_blocks):
    query_full = query_head.astype(jnp.float32)[None]
    value_full = payload_channel.astype(jnp.float32)[None]
    key_unit = unit_rows(key_head.astype(jnp.float32)[None])
    log_gate = gate_head[None]
    write_rate = rate_head[None]

    def forward_part(query_part, value_part):
        return block_core(query_part, value_part, key_unit, log_gate, write_rate)
    (written, query_eff, local_out), pullback, transition = jax.vjp(forward_part, query_full, value_full, has_aux=True)
    keep_four = keep_blocks[None, :, None, None]
    trans_kept = transition * keep_four
    writes_kept = written * keep_four
    grad_full = head_gradient.astype(jnp.float32)[None]
    block_count = query_head.shape[0]
    bit_count = block_count.bit_length() - 1
    weight_list = [weight_head[1 + level][None] for level in range(bit_count)]
    prefix_map, range_trans, range_state, out_extra, grad_extra, saved = fenwick_forward(trans_kept, writes_kept, query_eff, grad_full, weight_list, bit_count)
    top_grad = final_head[None, None]
    write_grads = fenwick_backward(top_grad, saved)
    level_zero = weight_head[0][None][..., None]
    head_out = level_zero * local_out + out_extra
    grad_query, grad_value = pullback((write_grads * keep_four, grad_extra, level_zero * grad_full))
    return (head_out[0], grad_query[0], grad_value[0])

def reference(queries, keys, values, log_decay, beta, level_weights, document_ends, out_weight, grad_y, final_state_grad):
    block_count = STREAM_POSITIONS // BLOCK
    grad_attn = jnp.dot(grad_y.astype(jnp.float32), out_weight.T.astype(jnp.float32), preferred_element_type=jnp.float32).astype(jnp.bfloat16)

    def by_heads(matrix):
        return matrix.reshape(block_count, BLOCK, HEADS, DK).transpose(2, 0, 1, 3)

    def by_tokens(stack):
        return stack.transpose(1, 2, 0, 3).reshape(STREAM_POSITIONS, HEADS * DK)
    keep_blocks = (1 - document_ends).astype(jnp.float32)
    gates = log_decay.reshape(HEADS, block_count, BLOCK)
    rates = beta.reshape(HEADS, block_count, BLOCK)
    tier_coefficients = level_weights.reshape(LEVELS, HEADS, block_count, BLOCK).transpose(1, 0, 2, 3)

    def per_head(items):
        return one_head(items[0], items[1], items[2], items[3], items[4], items[5], items[6], items[7], keep_blocks)
    head_out, grad_query, grad_value = lax.map(per_head, (by_heads(queries), by_heads(keys), by_heads(values), gates, rates, tier_coefficients, by_heads(grad_attn), final_state_grad))
    attn = by_tokens(head_out).astype(jnp.bfloat16)
    group = HEADS * DK // N_HEAD
    total = jnp.zeros((STREAM_POSITIONS, D), jnp.float32)
    for member in range(N_HEAD):
        partial_out = jnp.dot(attn[:, member * group:(member + 1) * group].astype(jnp.float32), out_weight[member * group:(member + 1) * group].astype(jnp.float32), preferred_element_type=jnp.float32)
        rounded = lax.optimization_barrier(partial_out.astype(jnp.bfloat16))
        total = total + rounded.astype(jnp.float32)
    layer_out = total.astype(jnp.bfloat16)
    return (layer_out, by_tokens(grad_query).astype(jnp.bfloat16), by_tokens(grad_value).astype(jnp.bfloat16))
```

```python
import jax
import jax.numpy as jnp
from jax import lax
from jax.experimental import pallas as pl
from jax.experimental.pallas import tpu as pltpu
from jax.sharding import PartitionSpec as P

F32 = jnp.float32
BF = jnp.bfloat16
NN = (((1,), (0,)), ((), ()))
NT = (((1,), (1,)), ((), ()))
TIERS = 7
SCAL = 32
SOME_VMEM = 16 * 1024 * 1024
MOST_VMEM = 63_000_000


SIZES = (("a", 1024), ("a2", 512), ("a4", 256), ("s", 1536), ("m", 1024), ("w", 512), ("u", 512), ("inv", 512),
         ("p", 512), ("e", 512), ("qe", 512), ("kt", 512), ("qn", 512), ("ks", 512))
STARTS = {}
KEPT = 0
for name, rows in SIZES:
    STARTS[name] = KEPT
    KEPT += rows
READS = [(c, n) for c in range(8) for n in (1, 2, 3) if c >> (n - 1) & 1]


def at(name, index, rows=128):
    start = STARTS[name] + index * rows
    return slice(start, start + rows)


def mm(a, b, dims=NN):
    return lax.dot_general(a, b, dims, preferred_element_type=F32)


def split(x):
    hi = x.astype(BF)
    return hi, (x - hi.astype(F32)).astype(BF)


def dot1(a, b, dims=NN):
    return mm(a.astype(BF), b.astype(BF), dims)


def dot3(a, b, dims=NN):
    ah, al = split(a)
    bh, bl = split(b)
    return mm(ah, bh, dims) + (mm(ah, bl, dims) + mm(al, bh, dims))


def dot2(a, b, dims=NN):
    ah, al = split(a)
    return mm(ah, b, dims) + mm(al, b, dims)


def tn(a, b, dot):
    return dot(a.T, b)


def iotas(rows, cols):
    return (
        lax.broadcasted_iota(jnp.int32, (rows, cols), 0),
        lax.broadcasted_iota(jnp.int32, (rows, cols), 1),
    )


def call(us, body, out_shapes, ins, scratch=(), fetch=False):
    count, outs = len(ins), len(out_shapes)
    big = [n for n, a in enumerate(ins) if a.dtype != jnp.int32]

    def fetching(*refs):
        held = refs[count + outs : count + outs + len(big)]
        sems = refs[count + outs + len(big)]
        own = list(refs[:count])
        copies = []
        for n, index in enumerate(big):
            copies.append(pltpu.make_async_copy(refs[index], held[n], sems.at[n]))
            own[index] = held[n]
        for copy in copies:
            copy.start()
        for copy in copies:
            copy.wait()
        body(*own, *refs[count : count + outs], *refs[count + outs + len(big) + 1 :])

    space = pltpu.HBM if fetch else pltpu.VMEM
    extra = [pltpu.VMEM(ins[n].shape, ins[n].dtype) for n in big] + [pltpu.SemaphoreType.DMA((len(big),))]
    return pl.pallas_call(
        fetching if fetch else body,
        out_shape=[jax.ShapeDtypeStruct(s, d) for s, d in out_shapes],
        in_specs=[pl.BlockSpec(memory_space=pltpu.SMEM if a.dtype == jnp.int32 else space) for a in ins],
        out_specs=[pl.BlockSpec(memory_space=pltpu.VMEM)] * outs,
        scratch_shapes=(extra if fetch else []) + list(scratch),
        cost_estimate=pl.CostEstimate(flops=int(us * 1.15e9), bytes_accessed=0, transcendentals=0),
        compiler_params=pltpu.CompilerParams(vmem_limit_bytes=MOST_VMEM if fetch else SOME_VMEM),
    )(*ins)


def pack_body(wh, ends, q, k, v, gy, gate, rate, tiers, *rest):
    outs, scal = rest[:-1], rest[-1]
    own, core = wh[4], wh[5]
    lane = lax.broadcasted_iota(jnp.int32, (1, 128), 1)
    keep = jnp.where(
        lane < 64, 1.0 - ends[0].astype(F32), 1.0 - ends[1].astype(F32)
    )

    def put(row, value, parts):
        for part in range(parts):
            piece = value.astype(BF).astype(F32)
            scal[row + part : row + part + 1, :] = piece
            value = value - piece

    for m in range(4):
        j = own ^ m
        cols = pl.ds(pl.multiple_of(j * 128, 128), 128)
        gcols = pl.ds(pl.multiple_of((j ^ (2 * core)) * 128, 128), 128)
        scal[...] = jnp.zeros((SCAL, 128), F32)
        put(0, gate[pl.ds(j, 1), :], 3)
        put(3, rate[pl.ds(j, 1), :], 2)
        for tier in range(TIERS):
            put(5 + 2 * tier, tiers[tier, pl.ds(j, 1), :], 2)
        scal[19:20, :] = keep
        outs[m][0:128, :] = k[:, cols]
        outs[m][128:256, :] = v[:, cols]
        outs[m][256:288, :] = scal[...].astype(BF)
        outs[m][288:416, :] = q[:, cols]
        outs[m][416:544, :] = gy[:, gcols]


def collect_body(p0, p1, p2, p3, out):
    for m, p in enumerate((p0, p1, p2, p3)):
        out[128 * m : 128 * m + 128, :] = p[416:544, :]


def join_body(p0, p1, p2, p3, out):
    for m, p in enumerate((p0, p1, p2, p3)):
        out[512 * m : 512 * m + 512, :] = p[...]


def block_body(wh, a0, a1, a2, a3, w0, ab_out, abf_out, far_out, kept, pack):
    del w0
    zlo = wh[0]
    for m, a in enumerate((a0, a1, a2, a3)):
        pack[pl.ds(zlo ^ m, 1)] = a[0:416, :][None]
    row, col = iotas(128, 128)
    same = (row >> 6) == (col >> 6)
    causal = same & (row >= col)
    strict = same & (row > col)
    eye = row == col
    eyef = eye.astype(F32)
    lblk = causal.astype(BF)
    top = row < 64
    trans, writes, local, qeff = [], [], [], []
    for i in range(4):
        k = pack[i, 0:128, :]
        v = pack[i, 128:256, :]
        scal = pack[i, 256:288, :]
        q = pack[i, 288:416, :]
        scalf = scal.astype(F32)
        cum3 = mm(lblk, scal, NT)
        cols = mm(eyef.astype(BF), scal, NT)
        cum_col = cum3[:, 0:1] + cum3[:, 1:2] + cum3[:, 2:3]
        cumr = mm(scal, lblk, NT)
        cum_row = cumr[0:1] + cumr[1:2] + cumr[2:3]
        beta_col = cols[:, 3:4] + cols[:, 4:5]
        beta_row = scalf[3:4] + scalf[4:5]
        kf, qf = k.astype(F32), q.astype(F32)
        rk_col = lax.rsqrt(jnp.sum(kf * kf, 1, keepdims=True) + 1e-6)
        rq_col = lax.rsqrt(jnp.sum(qf * qf, 1, keepdims=True) + 1e-6)
        rk_row = jnp.sum(jnp.where(eye, rk_col, 0.0), 0, keepdims=True)
        decay = jnp.where(causal, jnp.exp(jnp.where(causal, cum_col - cum_row, 0.0)), 0.0)
        kept[at("e", i), :] = decay
        gram = mm(k, k, NT)
        lower = jnp.where(strict, (beta_col * rk_col) * decay * (gram * rk_row), 0.0)
        inv = eyef - jnp.where((row >> 1) == (col >> 1), lower, 0.0)
        for bit in range(1, 6):
            near = ((row >> (bit + 1)) == (col >> (bit + 1))) & ((row >> bit) != (col >> bit))
            inv = inv - dot3(dot3(inv, jnp.where(near, lower, 0.0)), inv)
        kept[at("inv", i), :] = inv
        exp_col = jnp.exp(cum_col)
        w = dot2(inv * (beta_row * jnp.exp(cum_row) * rk_row), k)
        u = dot2(inv * beta_row, v)
        wu = jnp.concatenate([w, u], 1)
        kept[at("w", i), :] = w
        kept[at("u", i), :] = u
        last0, last1 = cum_row[:, 63:64], cum_row[:, 127:128]
        tail = jnp.exp(jnp.where(top[:, 0:1], last0, last1) - cum_col) * rk_col
        kept[at("kt", i), :] = tail * kf
        rhs = wu * tail
        top2 = lax.broadcasted_iota(jnp.int32, (128, 256), 0) < 64
        rhs = jnp.concatenate([jnp.where(top2, rhs, 0.0), jnp.where(top2, 0.0, rhs)], 1)
        rh, rl = split(rhs)
        kt = kf.T.astype(BF)
        ab = mm(kt, rh) + mm(kt, rl)
        for b, last in ((0, last0), (1, last1)):
            keep = scalf[19:20, 64 * b : 64 * b + 1]
            trans.append(keep * (jnp.exp(last) * eyef - ab[:, 256 * b : 256 * b + 128]))
            writes.append(keep * ab[:, 256 * b + 128 : 256 * b + 256])
        scores = decay * (mm(q, k, NT) * (rq_col * rk_row))
        kept[at("p", i), :] = scores
        pw = dot3(scores, wu)
        qn = rq_col * qf
        qe = exp_col * qn - pw[:, 0:128]
        kept[at("qe", i), :] = qe
        kept[at("qn", i), :] = qn
        kept[at("ks", i), :] = rk_col * kf
        weights = [cols[:, 5 + 2 * n : 6 + 2 * n] + cols[:, 6 + 2 * n : 7 + 2 * n] for n in range(TIERS)]
        far_out[i * 128 : (i + 1) * 128, :] = jnp.concatenate(
            weights + [cols[:, 19:20], rq_col, exp_col, beta_col, jnp.zeros((128, 128 - TIERS - 4), F32)], 1
        )
        local.append(pw[:, 128:256])
        qeff.append(qe)

    def both(a, x, y):
        r = dot3(a, jnp.concatenate([x, y], 1))
        return r[:, 0:128], r[:, 128:256]

    for c in range(8):
        kept[at("a", c), :] = trans[c]
    t2, w2 = [], []
    for p in range(4):
        t, s = both(trans[2 * p + 1], trans[2 * p], writes[2 * p])
        t2.append(t)
        w2.append(s + writes[2 * p + 1])
        kept[at("a2", p), :] = t
    t4, w4, map3, read3 = [], [], [], []
    for h in range(2):
        t, s = both(t2[2 * h + 1], t2[2 * h], w2[2 * h])
        t4.append(t)
        w4.append(s + w2[2 * h + 1])
        kept[at("a4", h), :] = t
        t, s = both(trans[4 * h + 2], t2[2 * h], w2[2 * h])
        map3.append(t)
        read3.append(s)
    tg, sg = both(t4[1], t4[0], w4[0])
    sg = sg + w4[1]
    ab_out[0:128, :] = tg.astype(BF)
    ab_out[128:256, :] = sg.astype(BF)
    abf_out[0:128, :] = tg
    abf_out[128:256, :] = sg
    maps = [eyef, trans[0], t2[0], map3[0], t4[0]]
    upper = [w4[0]]
    for inner in (trans[4], t2[2], map3[1]):
        t, s = both(inner, t4[0], w4[0])
        maps.append(t)
        upper.append(s)
    for c in range(8):
        kept[at("m", c), :] = maps[c]
        parts = []
        if c & 1:
            parts.append((1, writes[c - 1]))
        if c & 2:
            parts.append((2, w2[2 * (c >> 2)] if not c & 1 else read3[c >> 2]))
        if c & 4:
            parts.append((3, upper[c - 4]))
        rows = slice(64 * (c & 1), 64 * (c & 1) + 64)
        for level, state in parts:
            kept[at("s", READS.index((c, level))), :] = state
        rhs = jnp.concatenate([state for _, state in parts] + [maps[c]], 1)
        read = dot3(qeff[c >> 1][rows], rhs)
        weights = far_out[64 * c : 64 * c + 64, :]
        out = weights[:, 0:1] * local[c >> 1][rows]
        for n, (level, _) in enumerate(parts):
            out = out + weights[:, level : level + 1] * read[:, 128 * n : 128 * n + 128]
        far_out[1024 + 64 * c : 1024 + 64 * c + 64, :] = out
        far_out[512 + 64 * c : 512 + 64 * c + 64, :] = read[:, 128 * len(parts) :]


def pair_body(wh, own, other, bf_out, f_out, omap_out):
    up = wh[1] == 1
    o = other[...].astype(F32)
    mine = own[...]
    low = jnp.where(up, o, mine)
    high = jnp.where(up, mine, o)
    both = dot3(high[0:128], jnp.concatenate([low[0:128], low[128:256]], 1))
    t = both[:, 0:128]
    s = both[:, 128:256] + high[128:256]
    f_out[0:128, :] = t
    f_out[128:256, :] = s
    bf_out[0:128, :] = t.astype(BF)
    bf_out[128:256, :] = s.astype(BF)
    row, col = iotas(128, 128)
    omap_out[0:128, :] = jnp.where(up, low[0:128], (row == col).astype(F32))
    omap_out[128:256, :] = jnp.where(up, low[128:256], 0.0)


def far_body(wh, own, r1, r2, r3, omap, held, final, attn_out, s_out, up_out, fin_out, order):
    y = wh[2]
    for n, r in enumerate((own, r1, r2, r3)):
        order[pl.ds(y ^ n, 1)] = r[...].astype(F32)[None]
    up_out[...] = order[:, 0:128, :]
    o = omap[0:128, :]
    b5 = order[pl.ds(y ^ 1, 1)][0][128:256]
    b01 = dot3(order[1, 0:128, :], order[0, 128:256, :]) + order[1, 128:256, :]
    b6 = jnp.where(y == 3, dot3(order[2, 0:128, :], b01), b01)
    both = dot3(o, jnp.concatenate([jnp.where((y & 1) == 1, b5, 0.0), jnp.where(y >= 2, b6, 0.0)], 1))
    states = jnp.concatenate([omap[128:256, :], both], 1)
    s_out[...] = states
    read = dot3(held[512:1024, :], states)
    out = held[1024:1536, :]
    for n in range(3):
        out = out + held[0:512, 4 + n : 5 + n] * read[:, 128 * n : 128 * n + 128]
    attn_out[...] = out.astype(BF)
    f = final[pl.ds(wh[4], 1)][0]
    for j in (3, 2, 1):
        f = jnp.where(y < j, tn(order[j, 0:128, :], f, dot3), f)
    fin_out[...] = f


def pair_join_body(p0, p1, out):
    out[0:512, :] = p0[...]
    out[512:1024, :] = p1[...]


def order_weight(wh, parts, held):
    for n, part in enumerate(parts):
        for t in range(2):
            hb = 2 * (wh[2] ^ n) + (wh[1] ^ t)
            held[pl.ds(hb, 1)] = part[512 * t : 512 * t + 512, :][None]


def back_product_body(wh, ga, gb, w0, w1, w2, w3, own_out, o1, o2, o3, held):
    order_weight(wh, (w0, w1, w2, w3), held)
    total = None
    for n in range(4):
        for core, g in enumerate((ga, gb)):
            hb = wh[3] ^ (2 * n + core)
            w = held[pl.ds(hb, 1)][0]
            part = mm(g[512 * n : 512 * n + 512, :], w, NT)
            total = part if total is None else total + part
    acc = total
    for j in range(4):
        piece = acc[:, 128 * j : 128 * j + 128]

        for m, out in enumerate((own_out, o1, o2, o3)):

            @pl.when((wh[4] ^ m) == j)
            def _(piece=piece, out=out):
                out[...] = piece.astype(out.dtype)


def reach_body(wh, own, r1, r2, r3, held, omap, do_out, z5_out, z6_out, x4_out):
    for m in range(4):
        total = own[128 * m : 128 * m + 128, :]
        for k, r in ((1, r1), (2, r2), (3, r3)):
            total = total + r[128 * (m ^ k) : 128 * (m ^ k) + 128, :].astype(F32)
        do_out[pl.ds(wh[0] ^ m, 1)] = total.astype(BF)[None]
    do = do_out[...].reshape(512, 128).astype(F32)
    weighted = []
    for n in range(3):
        weighted.append(held[0:512, 4 + n : 5 + n] * do)
    x = tn(held[512:1024, :], jnp.concatenate(weighted, 1), dot3)
    x4_out[...] = jnp.where(wh[1] == 1, x[:, 0:128], 0.0)
    z = tn(omap[0:128, :], x[:, 128:384], dot3)
    z5_out[...] = z[:, 0:128].astype(BF)
    z6_out[...] = z[:, 128:256].astype(BF)


def grad_body(wh, do, held, far, kept, dq_out, dv_out, gmap_out):
    def weight(c, level):
        return held[64 * c : 64 * c + 64, level : level + 1]

    dof = do[...].reshape(512, 128).astype(F32)
    wd = [held[0:512, 4 + n : 5 + n] * dof for n in range(3)]
    carried = dot3(jnp.concatenate(wd, 1), far[...], NT)
    reach = {}
    dqe = []
    for c in range(8):
        rows = slice(64 * (c & 1), 64 * (c & 1) + 64)
        doc = do[c >> 1, rows, :].astype(F32)
        levels = [n for n in (1, 2, 3) if c >> (n - 1) & 1]
        left = jnp.concatenate([weight(c, n) * doc for n in levels] + [carried[64 * c : 64 * c + 64]], 1)
        right = jnp.concatenate(
            [kept[at("s", READS.index((c, n))), :] for n in levels] + [kept[at("m", c), :]], 1
        )
        dqe.append(dot3(left, right, NT))
        if levels:
            r = tn(kept[at("qe", c, 64), :], left[:, 0 : 128 * len(levels)], dot3)
            for n, level in enumerate(levels):
                reach[c, level] = r[:, 128 * n : 128 * n + 128]
    for i in range(4):
        doc = do[i].astype(F32)
        rows = slice(128 * i, 128 * i + 128)
        dqei = jnp.concatenate([dqe[2 * i], dqe[2 * i + 1]], 0)
        wu = jnp.concatenate([kept[at("w", i), :], kept[at("u", i), :]], 1)
        dp = dot3(jnp.concatenate([-dqei, held[rows, 0:1] * doc], 1), wu, NT) * kept[at("e", i), :]
        dqn = held[rows, 9:10] * dqei + dot3(dp, kept[at("ks", i), :])
        q = kept[at("qn", i), :]
        dq_out[i] = (held[rows, 8:9] * (dqn - q * jnp.sum(q * dqn, 1, keepdims=True))).astype(BF)
    row, col = iotas(128, 128)
    eyef = (row == col).astype(F32)

    def tnn(name, index, y):
        return tn(kept[at(name, index), :], y, dot3)

    d4 = reach[4, 3] + tnn("a", 4, reach[5, 3]) + tnn("a2", 2, reach[6, 3] + tnn("a", 6, reach[7, 3]))
    pair = {
        3: None,
        2: reach[6, 2] + tnn("a", 6, reach[7, 2]),
        1: d4,
        0: reach[2, 2] + tnn("a", 2, reach[3, 2]) + tnn("a2", 1, d4),
    }
    a4 = kept[at("a4", 1), :]
    suf = {3: eyef, 2: kept[at("a2", 3), :], 1: a4, 0: dot3(a4, kept[at("a2", 1), :])}
    for i in range(4):
        odd = pair[i]
        even = reach[2 * i + 1, 1] if odd is None else reach[2 * i + 1, 1] + tnn("a", 2 * i + 1, odd)
        odd = jnp.zeros((128, 128), F32) if odd is None else odd
        s_odd = suf[i]
        s_even = dot3(s_odd, kept[at("a", 2 * i + 1), :])
        rows = slice(128 * i, 128 * i + 128)
        doc = do[i].astype(F32)
        pd = tn(kept[at("p", i), :], held[rows, 0:1] * doc, dot3)
        kk = held[rows, 7:8] * kept[at("kt", i), :]
        left = dot3(kk[0:64], jnp.concatenate([even, s_even.T], 1))
        right = dot3(kk[64:128], jnp.concatenate([odd, s_odd.T], 1))
        hn = jnp.concatenate([left, right], 0)
        both = jnp.concatenate([pd + hn[:, 0:128], hn[:, 128:256]], 1)
        both = held[rows, 10:11] * tn(kept[at("inv", i), :], both, dot3)
        dv_out[rows, :] = both[:, 0:128]
        gmap_out[rows, :] = both[:, 128:256]


def near_body(wh, r1, r2, r3, ups, own, fin, x4, send_out, keep_out):
    y = wh[2]
    up = wh[1] == 1
    a = r2[...].astype(F32)
    b = r3[...].astype(F32)
    second = jnp.where(y == 0, a, b)
    third = jnp.where(y == 0, b, a)
    d01 = second + tn(ups[2], third, dot3)
    d01 = jnp.where(y == 0, tn(ups[1], d01, dot3), jnp.where(y == 1, d01, 0.0))
    part = d01 + jnp.where((y & 1) == 0, r1[...].astype(F32), 0.0)
    trans = own[0:128, :]
    full = part + fin[...]
    pulled = tn(trans, part, dot3) + x4[...]
    send_out[...] = jnp.where(up, pulled, part).astype(BF)
    keep_out[...] = full


def value_body(wh, r, kept, other, dv, gmap, dq, o0, o1, o2, o3, dvs):
    up = wh[1] == 1
    got = r[...].astype(F32)
    pulled = tn(other[0:128, :].astype(F32), kept[...], dot3)
    g = got + jnp.where(up, kept[...], pulled)
    res = dv[...] + dot3(gmap[...], g)
    dvs[...] = res.astype(BF).reshape(4, 128, 128)
    for m, out in enumerate((o0, o1, o2, o3)):
        out[0:128, :] = dq[pl.ds(wh[0] ^ m, 1)][0]
        out[128:256, :] = dvs[pl.ds(wh[0] ^ m, 1)][0]


def project_body(wh, a0, a1, a2, a3, w0, w1, w2, w3, even, odd, held):
    order_weight(wh, (w0, w1, w2, w3), held)
    for n in range(8):
        total = None
        for m, a in enumerate((a0, a1, a2, a3)):
            rows = pl.ds(pl.multiple_of((wh[4] ^ m) * 128, 128), 128)
            w = held[pl.ds(wh[3] ^ n, 1), rows, :][0]
            part = mm(a[...], w)
            total = part if total is None else total + part
        out = odd if n & 1 else even
        out[512 * (n >> 1) : 512 * (n >> 1) + 512, :] = total.astype(BF)


def sum_pair_body(own, r, f_out, o2, o4, o6):
    f_out[...] = own[0:512, :].astype(F32) + r[0:512, :].astype(F32)
    for n, out in ((1, o2), (2, o4), (3, o6)):
        rows = slice(512 * n, 512 * n + 512)
        out[...] = (own[rows, :].astype(F32) + r[rows, :].astype(F32)).astype(BF)


def sum_last_body(wh, f, r2, r4, r6, o0, o1, o2, o3, done):
    total = f[...] + r2[...].astype(F32) + r4[...].astype(F32) + r6[...].astype(F32)
    done[...] = total.astype(BF).reshape(4, 128, 128)
    for m, out in enumerate((o0, o1, o2, o3)):
        out[...] = done[pl.ds(wh[0] ^ m, 1)][0]


def place_heads_body(wh, r0, r1, r2, r3, dq, dv):
    for m, r in enumerate((r0, r1, r2, r3)):
        cols = pl.ds(pl.multiple_of((wh[4] ^ m) * 128, 128), 128)
        dq[:, cols] = r[0:128, :]
        dv[:, cols] = r[128:256, :]


def place_columns_body(wh, r0, r1, r2, r3, out):
    for m, r in enumerate((r0, r1, r2, r3)):
        j = wh[4] ^ m ^ (2 * wh[5])
        out[:, pl.ds(pl.multiple_of(j * 128, 128), 128)] = r[...]


def xor(value, axis, mask):
    return lax.ppermute(value, axis, [(s, s ^ mask) for s in range(lax.axis_size(axis))])


def own_head(z):
    return (z & 3) ^ (2 * (z >> 2))


def shards(queries, keys, values, log_decay, beta, level_weights, document_ends, out_weight, grad_y, final_state_grad):
    s = lax.axis_index("seq")
    h = lax.axis_index("head")
    z = s & 7
    where = jnp.stack([z & 3, z >> 2, s >> 3, h, own_head(z), h & 1, 0 * h, 0 * h]).astype(jnp.int32)
    wz = xor(out_weight, "seq", 6)
    w0 = call(1, pair_join_body, [((1024, 128), BF)], [out_weight, wz])[0]
    weight = [w0] + [xor(w0, "seq", 8 * n) for n in (1, 2, 3)]

    packs = call(
        3, pack_body,
        [((544, 128), BF)] * 4,
        [where, document_ends, queries, keys, values, grad_y, log_decay, beta, level_weights],
        [pltpu.VMEM((SCAL, 128), F32)],
        fetch=True,
    )
    mine = [packs[0]] + [xor(packs[m], "seq", m) for m in (1, 2, 3)]
    gm = call(1, collect_body, [((512, 128), BF)], mine)[0]
    ga = [gm] + [xor(gm, "head", 2 * n) for n in (1, 2, 3)]

    T = (512, 128)
    S = (128, 128)
    ab, abf, held, kept = call(
        11, block_body,
        [((256, 128), BF), ((256, 128), F32), ((1536, 128), F32), ((KEPT, 128), F32)],
        [where] + mine + [w0],
        [pltpu.VMEM((4, 416, 128), BF)],
    )
    other = xor(ab, "seq", 6)
    gj = call(1, join_body, [((2048, 128), BF)], ga)[0]
    gb = xor(gj, "head", 1)
    pair_bf, pair_f, omap = call(
        1, pair_body, [((256, 128), BF), ((256, 128), F32), ((256, 128), F32)], [where, abf, other]
    )
    far = [xor(pair_bf, "seq", 8 * n) for n in (1, 2, 3)]
    attn, far_states, ups, fin = call(
        2, far_body,
        [(T, BF), ((128, 384), F32), ((4,) + S, F32), (S, F32)],
        [where, pair_f] + far + [omap, held, final_state_grad],
        [pltpu.VMEM((4, 256, 128), F32)],
    )

    back = call(3, back_product_body, [(T, F32), (T, BF), (T, BF), (T, BF)], [where, gj, gb] + weight, [pltpu.VMEM((8, 512, 128), BF)])
    rb = [xor(back[m], "seq", m) for m in (1, 2, 3)]
    do, z5, z6, x4 = call(
        2, reach_body, [((4,) + S, BF), (S, BF), (S, BF), (S, F32)], [where, back[0]] + rb + [held, omap]
    )
    near = [xor(z5, "seq", 8), xor(z6, "seq", 16), xor(z6, "seq", 24)]
    dq, dv_part, gmap = call(
        7, grad_body, [((4,) + S, BF), (T, F32), (T, F32)], [where, do, held, far_states, kept]
    )
    send, local = call(1, near_body, [(S, BF), (S, F32)], [where] + near + [ups, abf, fin, x4])
    got = xor(send, "seq", 6)
    dqv = call(
        1, value_body, [((256, 128), BF)] * 4, [where, got, local, other, dv_part, gmap, dq], [pltpu.VMEM((4,) + S, BF)]
    )

    at = [attn] + [xor(attn, "seq", m) for m in (1, 2, 3)]
    even, odd = call(3, project_body, [((2048, 128), BF)] * 2, [where] + at + weight, [pltpu.VMEM((8, 512, 128), BF)])
    swapped = xor(odd, "head", 1)
    sums = call(1, sum_pair_body, [(T, F32), (T, BF), (T, BF), (T, BF)], [even, swapped])
    rx = [xor(sums[n], "head", 2 * n) for n in (1, 2, 3)]
    lo = call(1, sum_last_body, [(S, BF)] * 4, [where, sums[0]] + rx, [pltpu.VMEM((4,) + S, BF)])

    def home(parts):
        return [parts[0]] + [xor(parts[m], "seq", m) for m in (1, 2, 3)]

    whole = (128, 512)
    layer = call(1, place_columns_body, [(whole, BF)], [where] + home(lo))[0]
    grad_q, grad_v = call(1, place_heads_body, [(whole, BF)] * 2, [where] + home(dqv))
    return (layer, grad_q, grad_v)


def solution(mesh):
    in_specs = (
        P("seq", "head"),
        P("seq", "head"),
        P("seq", "head"),
        P("head", "seq"),
        P("head", "seq"),
        P(None, "head", "seq"),
        P("seq"),
        P("head", "seq"),
        P("seq", "head"),
        P("head", None, None),
    )
    out_specs = (P("seq", "head"), P("seq", "head"), P("seq", "head"))
    return jax.shard_map(shards, mesh=mesh, in_specs=in_specs, out_specs=out_specs, check_vma=False)
```

```python
import jax
import jax.numpy as jnp
from jax import lax
from jax.experimental import pallas as pl
from jax.experimental.pallas import tpu as pltpu
from jax.sharding import PartitionSpec as P

F32 = jnp.float32
BF = jnp.bfloat16
NN = (((1,), (0,)), ((), ()))
NT = (((1,), (1,)), ((), ()))
TIERS = 7
SCALE = 1e8
SCAL = 32
SOME_VMEM = 16 * 1024 * 1024
MOST_VMEM = 63_000_000


SIZES = (("a", 1024), ("a2", 512), ("a4", 256), ("s", 1536), ("m", 1024), ("w", 512), ("u", 512), ("inv", 512),
         ("er", 512), ("kt", 512), ("k", 512))
LATER = (("p", 512), ("qe", 512), ("qn", 512))
STARTS = {}


def lay(sizes):
    total = 0
    for name, rows in sizes:
        STARTS[name] = total
        total += rows
    return total


KEPT = lay(SIZES)
KEPT_LATER = lay(LATER)
READS = [(c, n) for c in range(8) for n in (1, 2, 3) if c >> (n - 1) & 1]


def at(name, index, rows=128):
    start = STARTS[name] + index * rows
    return slice(start, start + rows)


def mm(a, b, dims=NN):
    return lax.dot_general(a, b, dims, preferred_element_type=F32)


def split(x):
    hi = x.astype(BF)
    return hi, (x - hi.astype(F32)).astype(BF)


def stack(dims, a, b):
    return mm(jnp.concatenate(a, 1), jnp.concatenate(b, dims[0][1][0]), dims)


def dot3(a, b, dims=NN):
    ah, al = split(a)
    bh, bl = split(b)
    return stack(dims, [ah, al, ah], [bh, bh, bl])


def dot2(a, b, dims=NN):
    b = b.astype(BF)
    return stack(dims, split(a), [b, b])


TREE = dot3


def tn(a, b, dot):
    return dot(a.T, b)


def iotas(rows, cols):
    return (
        lax.broadcasted_iota(jnp.int32, (rows, cols), 0),
        lax.broadcasted_iota(jnp.int32, (rows, cols), 1),
    )


def call(us, body, out_shapes, ins, scratch=(), fetch=False, after=()):
    count, outs, waits = len(ins), len(out_shapes), len(after)
    big = [n for n, a in enumerate(ins) if a.dtype != jnp.int32]

    def fetching(*refs):
        held = refs[count + outs : count + outs + len(big)]
        sems = refs[count + outs + len(big)]
        own = list(refs[:count])
        copies = []
        for n, index in enumerate(big):
            copies.append(pltpu.make_async_copy(refs[index], held[n], sems.at[n]))
            own[index] = held[n]
        for copy in copies:
            copy.start()
        for copy in copies:
            copy.wait()
        body(*own, *refs[count : count + outs], *refs[count + outs + len(big) + 1 :])

    def waiting(*refs):
        (fetching if fetch else body)(*refs[:count], *refs[count + waits :])

    space = pltpu.HBM if fetch else pltpu.VMEM
    extra = [pltpu.VMEM(ins[n].shape, ins[n].dtype) for n in big] + [pltpu.SemaphoreType.DMA((len(big),))]
    with jax.named_scope(body.__name__.removesuffix("_body")):
        return pl.pallas_call(
            waiting,
            out_shape=[jax.ShapeDtypeStruct(s, d) for s, d in out_shapes],
            in_specs=[pl.BlockSpec(memory_space=pltpu.SMEM if a.dtype == jnp.int32 else space) for a in ins]
            + [pl.BlockSpec(memory_space=pl.ANY)] * waits,
            out_specs=[pl.BlockSpec(memory_space=pltpu.VMEM)] * outs,
            scratch_shapes=(extra if fetch else []) + list(scratch),
            cost_estimate=pl.CostEstimate(flops=int(us * SCALE), bytes_accessed=0, transcendentals=0),
            compiler_params=pltpu.CompilerParams(vmem_limit_bytes=MOST_VMEM if fetch else SOME_VMEM),
        )(*ins, *after)


def pack_body(wh, ends, q, k, v, gy, gate, rate, tiers, *rest):
    outs, scal = rest[:-1], rest[-1]
    own, core = wh[4], wh[5]
    lane = lax.broadcasted_iota(jnp.int32, (1, 128), 1)
    keep = jnp.where(
        lane < 64, 1.0 - ends[0].astype(F32), 1.0 - ends[1].astype(F32)
    )

    def put(row, value, parts):
        for part in range(parts):
            piece = value.astype(BF).astype(F32)
            scal[row + part : row + part + 1, :] = piece
            value = value - piece

    for m in range(4):
        j = own ^ m
        cols = pl.ds(pl.multiple_of(j * 128, 128), 128)
        gcols = pl.ds(pl.multiple_of((j ^ (2 * core)) * 128, 128), 128)
        scal[...] = jnp.zeros((SCAL, 128), F32)
        put(0, gate[pl.ds(j, 1), :], 3)
        put(3, rate[pl.ds(j, 1), :], 2)
        for tier in range(TIERS):
            put(5 + 2 * tier, tiers[tier, pl.ds(j, 1), :], 2)
        scal[19:20, :] = keep
        outs[m][0:128, :] = k[:, cols]
        outs[m][128:256, :] = v[:, cols]
        outs[m][256:288, :] = scal[...].astype(BF)
        outs[m][288:416, :] = q[:, cols]
        outs[m][416:544, :] = gy[:, gcols]


def collect_body(p0, p1, p2, p3, out):
    for m, p in enumerate((p0, p1, p2, p3)):
        out[128 * m : 128 * m + 128, :] = p[416:544, :]


def join_body(p0, p1, p2, p3, out):
    for m, p in enumerate((p0, p1, p2, p3)):
        out[512 * m : 512 * m + 512, :] = p[...]


def block_masks():
    row, col = iotas(128, 128)
    same = (row >> 6) == (col >> 6)
    return row, col, same & (row >= col), same & (row > col)


def gates(scal, lblk):
    cum3 = mm(lblk, scal, NT)
    eye = jnp.where(jnp.equal(*iotas(128, 128)), 1.0, 0.0).astype(BF)
    return cum3[:, 0:1] + cum3[:, 1:2] + cum3[:, 2:3], mm(eye, scal, NT)


def block_body(wh, a0, a1, a2, a3, ab_out, abf_out, kept, pack):
    zlo = wh[0]
    for m, a in enumerate((a0, a1, a2, a3)):
        pack[pl.ds(zlo ^ m, 1)] = a[0:288, :][None]
    row, col, causal, strict = block_masks()
    eye = row == col
    eyef = eye.astype(F32)
    lblk = causal.astype(BF)
    trans, writes = [], []
    for i in range(4):
        k = pack[i, 0:128, :]
        v = pack[i, 128:256, :]
        scal = pack[i, 256:288, :]
        scalf = scal.astype(F32)
        cum_col, cols = gates(scal, lblk)
        cumr = mm(scal, lblk, NT)
        cum_row = cumr[0:1] + cumr[1:2] + cumr[2:3]
        beta_col = cols[:, 3:4] + cols[:, 4:5]
        beta_row = scalf[3:4] + scalf[4:5]
        kf = k.astype(F32)
        rk_col = lax.rsqrt(jnp.sum(kf * kf, 1, keepdims=True) + 1e-6)
        rk_row = jnp.sum(jnp.where(eye, rk_col, 0.0), 0, keepdims=True)
        decay = rk_row * jnp.where(causal, jnp.exp(jnp.where(causal, cum_col - cum_row, 0.0)), 0.0)
        kept[at("er", i), :] = decay
        kept[at("k", i), :] = kf
        lower = jnp.where(strict, (beta_col * rk_col) * (decay * mm(k, k, NT)), 0.0)
        inv = eyef - jnp.where((row >> 1) == (col >> 1), lower, 0.0)
        for bit in range(1, 6):
            near = ((row >> (bit + 1)) == (col >> (bit + 1))) & ((row >> bit) != (col >> bit))
            inv = inv - dot3(dot3(inv, jnp.where(near, lower, 0.0)), inv)
        kept[at("inv", i), :] = inv
        w = dot2(inv * (beta_row * jnp.exp(cum_row) * rk_row), k)
        u = dot2(inv * beta_row, v)
        wu = jnp.concatenate([w, u], 1)
        kept[at("w", i), :] = w
        kept[at("u", i), :] = u
        last0, last1 = cum_row[:, 63:64], cum_row[:, 127:128]
        tail = jnp.exp(jnp.where(row[:, 0:1] < 64, last0, last1) - cum_col) * rk_col
        kept[at("kt", i), :] = tail * kf
        rhs = wu * tail
        top = lax.broadcasted_iota(jnp.int32, (128, 256), 0) < 64
        rhs = jnp.concatenate([jnp.where(top, rhs, 0.0), jnp.where(top, 0.0, rhs)], 1)
        kt = kf.T.astype(BF)
        ab = stack(NN, [kt, kt], split(rhs))
        for b, last in ((0, last0), (1, last1)):
            keep = scalf[19:20, 64 * b : 64 * b + 1]
            trans.append(keep * (jnp.exp(last) * eyef - ab[:, 256 * b : 256 * b + 128]))
            writes.append(keep * ab[:, 256 * b + 128 : 256 * b + 256])

    def both(a, x, y):
        r = TREE(a, jnp.concatenate([x, y], 1))
        return r[:, 0:128], r[:, 128:256]

    for c in range(8):
        kept[at("a", c), :] = trans[c]
    t2, w2 = [], []
    for p in range(4):
        t, s = both(trans[2 * p + 1], trans[2 * p], writes[2 * p])
        t2.append(t)
        w2.append(s + writes[2 * p + 1])
        kept[at("a2", p), :] = t
    t4, w4 = [], []
    for h in range(2):
        t, s = both(t2[2 * h + 1], t2[2 * h], w2[2 * h])
        t4.append(t)
        w4.append(s + w2[2 * h + 1])
        kept[at("a4", h), :] = t
    tg, sg = both(t4[1], t4[0], w4[0])
    sg = sg + w4[1]
    ab_out[0:128, :] = tg.astype(BF)
    ab_out[128:256, :] = sg.astype(BF)
    abf_out[0:128, :] = tg
    abf_out[128:256, :] = sg
    map3, read3 = [], []
    for h in range(2):
        t, s = both(trans[4 * h + 2], t2[2 * h], w2[2 * h])
        map3.append(t)
        read3.append(s)
    maps = [eyef, trans[0], t2[0], map3[0], t4[0]]
    upper = [w4[0]]
    for inner in (trans[4], t2[2], map3[1]):
        t, s = both(inner, t4[0], w4[0])
        maps.append(t)
        upper.append(s)
    for c in range(8):
        kept[at("m", c), :] = maps[c]
    for n, (c, level) in enumerate(READS):
        if level == 1:
            state = writes[c - 1]
        elif level == 2:
            state = read3[c >> 2] if c & 1 else w2[2 * (c >> 2)]
        else:
            state = upper[c - 4]
        kept[at("s", n), :] = state


def query_body(wh, a0, a1, a2, a3, kept, held, later, scals, qs):
    for m, a in enumerate((a0, a1, a2, a3)):
        scals[pl.ds(wh[0] ^ m, 1)] = a[256:288, :][None]
        qs[pl.ds(wh[0] ^ m, 1)] = a[288:416, :][None]
    lblk = block_masks()[2].astype(BF)
    for i in range(4):
        q = qs[i]
        qf = q.astype(F32)
        cum_col, cols = gates(scals[i], lblk)
        exp_col = jnp.exp(cum_col)
        rq_col = lax.rsqrt(jnp.sum(qf * qf, 1, keepdims=True) + 1e-6)
        scores = kept[at("er", i), :] * (rq_col * mm(q, kept[at("k", i), :].astype(BF), NT))
        later[at("p", i), :] = scores
        pw = dot2(scores, jnp.concatenate([kept[at("w", i), :], kept[at("u", i), :]], 1))
        qn = rq_col * qf
        qe = exp_col * qn - pw[:, 0:128]
        later[at("qe", i), :] = qe
        later[at("qn", i), :] = qn
        weights = [cols[:, 5 + 2 * n : 6 + 2 * n] + cols[:, 6 + 2 * n : 7 + 2 * n] for n in range(TIERS)]
        beta_col = cols[:, 3:4] + cols[:, 4:5]
        held[i * 128 : (i + 1) * 128, :] = jnp.concatenate(
            weights + [cols[:, 19:20], rq_col, exp_col, beta_col, jnp.zeros((128, 128 - TIERS - 4), F32)], 1
        )
        for c in (2 * i, 2 * i + 1):
            rows = slice(64 * (c & 1), 64 * (c & 1) + 64)
            levels = [n for n in (1, 2, 3) if c >> (n - 1) & 1]
            rhs = jnp.concatenate(
                [kept[at("s", READS.index((c, n))), :] for n in levels] + [kept[at("m", c), :]], 1
            )
            read = dot2(qe[rows], rhs)
            out = weights[0][rows] * pw[rows, 128:256]
            for n, level in enumerate(levels):
                out = out + weights[level][rows] * read[:, 128 * n : 128 * n + 128]
            held[1024 + 64 * c : 1024 + 64 * c + 64, :] = out
            held[512 + 64 * c : 512 + 64 * c + 64, :] = read[:, 128 * len(levels) :]


def pair_body(wh, own, other, bf_out, f_out, omap_out):
    up = wh[1] == 1
    o = other[...].astype(F32)
    mine = own[...]
    low = jnp.where(up, o, mine)
    high = jnp.where(up, mine, o)
    both = dot3(high[0:128], jnp.concatenate([low[0:128], low[128:256]], 1))
    t = both[:, 0:128]
    s = both[:, 128:256] + high[128:256]
    f_out[0:128, :] = t
    f_out[128:256, :] = s
    bf_out[0:128, :] = t.astype(BF)
    bf_out[128:256, :] = s.astype(BF)
    row, col = iotas(128, 128)
    omap_out[0:128, :] = jnp.where(up, low[0:128], (row == col).astype(F32))
    omap_out[128:256, :] = jnp.where(up, low[128:256], 0.0)


def far_body(wh, own, r1, r2, r3, omap, held, final, attn_out, s_out, up_out, fin_out, order):
    y = wh[2]
    for n, r in enumerate((own, r1, r2, r3)):
        order[pl.ds(y ^ n, 1)] = r[...].astype(F32)[None]
    up_out[...] = order[:, 0:128, :]
    o = omap[0:128, :]
    b5 = order[pl.ds(y ^ 1, 1)][0][128:256]
    b01 = dot3(order[1, 0:128, :], order[0, 128:256, :]) + order[1, 128:256, :]
    b6 = jnp.where(y == 3, dot3(order[2, 0:128, :], b01), b01)
    both = dot3(o, jnp.concatenate([jnp.where((y & 1) == 1, b5, 0.0), jnp.where(y >= 2, b6, 0.0)], 1))
    states = jnp.concatenate([omap[128:256, :], both], 1)
    s_out[...] = states
    read = dot3(held[512:1024, :], states)
    out = held[1024:1536, :]
    for n in range(3):
        out = out + held[0:512, 4 + n : 5 + n] * read[:, 128 * n : 128 * n + 128]
    attn_out[...] = out.astype(BF)
    f = final[pl.ds(wh[4], 1)][0]
    for j in (3, 2, 1):
        f = jnp.where(y < j, tn(order[j, 0:128, :], f, dot3), f)
    fin_out[...] = f


def join_weight_body(p0, p1, pack, out, own):
    out[0:512, :] = p0[...]
    out[512:1024, :] = p1[...]
    own[...] = pack[...]


def order_weight(wh, parts, held):
    for n, part in enumerate(parts):
        for t in range(2):
            hb = 2 * (wh[2] ^ n) + (wh[1] ^ t)
            held[pl.ds(hb, 1)] = part[512 * t : 512 * t + 512, :][None]


def back_product_body(wh, ga, gb, w0, w1, w2, w3, own_out, o1, o2, o3, held):
    order_weight(wh, (w0, w1, w2, w3), held)
    total = None
    for n in range(4):
        for core, g in enumerate((ga, gb)):
            hb = wh[3] ^ (2 * n + core)
            w = held[pl.ds(hb, 1)][0]
            part = mm(g[512 * n : 512 * n + 512, :], w, NT)
            total = part if total is None else total + part
    acc = total
    for j in range(4):
        piece = acc[:, 128 * j : 128 * j + 128]

        for m, out in enumerate((own_out, o1, o2, o3)):

            @pl.when((wh[4] ^ m) == j)
            def _(piece=piece, out=out):
                out[...] = piece.astype(out.dtype)


def reach_body(wh, own, r1, r2, r3, held, omap, do_out, z5_out, z6_out, x4_out):
    for m in range(4):
        total = own[128 * m : 128 * m + 128, :]
        for k, r in ((1, r1), (2, r2), (3, r3)):
            total = total + r[128 * (m ^ k) : 128 * (m ^ k) + 128, :].astype(F32)
        do_out[pl.ds(wh[0] ^ m, 1)] = total.astype(BF)[None]
    do = do_out[...].reshape(512, 128).astype(F32)
    weighted = []
    for n in range(3):
        weighted.append(held[0:512, 4 + n : 5 + n] * do)
    x = tn(held[512:1024, :], jnp.concatenate(weighted, 1), dot2)
    x4_out[...] = jnp.where(wh[1] == 1, x[:, 0:128], 0.0)
    z = tn(omap[0:128, :], x[:, 128:384], dot2)
    z5_out[...] = z[:, 0:128].astype(BF)
    z6_out[...] = z[:, 128:256].astype(BF)


def grad_body(wh, do, held, far, kept, later, dq_out, dv_out, gmap_out):
    def weight(c, level):
        return held[64 * c : 64 * c + 64, level : level + 1]

    dof = do[...].reshape(512, 128).astype(F32)
    wd = [held[0:512, 4 + n : 5 + n] * dof for n in range(3)]
    carried = dot2(jnp.concatenate(wd, 1), far[...], NT)
    reach = {}
    dqe = []
    for c in range(8):
        rows = slice(64 * (c & 1), 64 * (c & 1) + 64)
        doc = do[c >> 1, rows, :].astype(F32)
        levels = [n for n in (1, 2, 3) if c >> (n - 1) & 1]
        left = jnp.concatenate([weight(c, n) * doc for n in levels] + [carried[64 * c : 64 * c + 64]], 1)
        right = jnp.concatenate(
            [kept[at("s", READS.index((c, n))), :] for n in levels] + [kept[at("m", c), :]], 1
        )
        dqe.append(dot2(left, right, NT))
        if levels:
            r = tn(later[at("qe", c, 64), :], left[:, 0 : 128 * len(levels)], dot2)
            for n, level in enumerate(levels):
                reach[c, level] = r[:, 128 * n : 128 * n + 128]
    for i in range(4):
        doc = do[i].astype(F32)
        rows = slice(128 * i, 128 * i + 128)
        dqei = jnp.concatenate([dqe[2 * i], dqe[2 * i + 1]], 0)
        wu = jnp.concatenate([kept[at("w", i), :], kept[at("u", i), :]], 1)
        dp = dot2(jnp.concatenate([-dqei, held[rows, 0:1] * doc], 1), wu, NT) * kept[at("er", i), :]
        dqn = held[rows, 9:10] * dqei + dot2(dp, kept[at("k", i), :])
        q = later[at("qn", i), :]
        dq_out[i] = (held[rows, 8:9] * (dqn - q * jnp.sum(q * dqn, 1, keepdims=True))).astype(BF)
    row, col = iotas(128, 128)
    eyef = (row == col).astype(F32)

    def tnn(name, index, y):
        return tn(kept[at(name, index), :], y, dot3)

    d4 = reach[4, 3] + tnn("a", 4, reach[5, 3]) + tnn("a2", 2, reach[6, 3] + tnn("a", 6, reach[7, 3]))
    pair = {
        3: None,
        2: reach[6, 2] + tnn("a", 6, reach[7, 2]),
        1: d4,
        0: reach[2, 2] + tnn("a", 2, reach[3, 2]) + tnn("a2", 1, d4),
    }
    a4 = kept[at("a4", 1), :]
    suf = {3: eyef, 2: kept[at("a2", 3), :], 1: a4, 0: dot3(a4, kept[at("a2", 1), :])}
    for i in range(4):
        odd = pair[i]
        even = reach[2 * i + 1, 1] if odd is None else reach[2 * i + 1, 1] + tnn("a", 2 * i + 1, odd)
        odd = jnp.zeros((128, 128), F32) if odd is None else odd
        s_odd = suf[i]
        s_even = dot3(s_odd, kept[at("a", 2 * i + 1), :])
        rows = slice(128 * i, 128 * i + 128)
        doc = do[i].astype(F32)
        pd = tn(later[at("p", i), :], held[rows, 0:1] * doc, dot3)
        kk = held[rows, 7:8] * kept[at("kt", i), :]
        left = dot3(kk[0:64], jnp.concatenate([even, s_even.T], 1))
        right = dot3(kk[64:128], jnp.concatenate([odd, s_odd.T], 1))
        hn = jnp.concatenate([left, right], 0)
        both = jnp.concatenate([pd + hn[:, 0:128], hn[:, 128:256]], 1)
        both = held[rows, 10:11] * tn(kept[at("inv", i), :], both, dot3)
        dv_out[rows, :] = both[:, 0:128]
        gmap_out[rows, :] = both[:, 128:256]


def near_body(wh, r1, r2, r3, ups, own, fin, x4, send_out, keep_out):
    y = wh[2]
    up = wh[1] == 1
    a = r2[...].astype(F32)
    b = r3[...].astype(F32)
    second = jnp.where(y == 0, a, b)
    third = jnp.where(y == 0, b, a)
    d01 = second + tn(ups[2], third, dot3)
    d01 = jnp.where(y == 0, tn(ups[1], d01, dot3), jnp.where(y == 1, d01, 0.0))
    part = d01 + jnp.where((y & 1) == 0, r1[...].astype(F32), 0.0)
    trans = own[0:128, :]
    full = part + fin[...]
    pulled = tn(trans, part, dot3) + x4[...]
    send_out[...] = jnp.where(up, pulled, part).astype(BF)
    keep_out[...] = full


def value_body(wh, r, kept, other, dv, gmap, out):
    up = wh[1] == 1
    got = r[...].astype(F32)
    pulled = tn(other[0:128, :].astype(F32), kept[...], dot3)
    g = got + jnp.where(up, kept[...], pulled)
    res = dv[...] + dot3(gmap[...], g)
    out[...] = res.astype(BF).reshape(4, 128, 128)


def project_body(wh, a0, a1, a2, a3, w0, w1, w2, w3, even, odd, held):
    order_weight(wh, (w0, w1, w2, w3), held)
    for n in range(8):
        total = None
        for m, a in enumerate((a0, a1, a2, a3)):
            rows = pl.ds(pl.multiple_of((wh[4] ^ m) * 128, 128), 128)
            w = held[pl.ds(wh[3] ^ n, 1), rows, :][0]
            part = mm(a[...], w)
            total = part if total is None else total + part
        out = odd if n & 1 else even
        out[512 * (n >> 1) : 512 * (n >> 1) + 512, :] = total.astype(BF)


def sum_pair_body(own, r, f_out, o2, o4, o6):
    f_out[...] = own[0:512, :].astype(F32) + r[0:512, :].astype(F32)
    for n, out in ((1, o2), (2, o4), (3, o6)):
        rows = slice(512 * n, 512 * n + 512)
        out[...] = (own[rows, :].astype(F32) + r[rows, :].astype(F32)).astype(BF)


def sum_last_body(wh, f, r2, r4, r6, dq, dv, o0, o1, o2, o3, done):
    total = f[...] + r2[...].astype(F32) + r4[...].astype(F32) + r6[...].astype(F32)
    done[...] = total.astype(BF).reshape(4, 128, 128)
    for m, out in enumerate((o0, o1, o2, o3)):
        for n, part in enumerate((done, dq, dv)):
            out[128 * n : 128 * n + 128, :] = part[pl.ds(wh[0] ^ m, 1)][0]


def place_body(wh, r0, r1, r2, r3, layer, dq, dv):
    for m, r in enumerate((r0, r1, r2, r3)):
        j = wh[4] ^ m
        cols = pl.ds(pl.multiple_of(j * 128, 128), 128)
        layer[:, pl.ds(pl.multiple_of((j ^ (2 * wh[5])) * 128, 128), 128)] = r[0:128, :]
        dq[:, cols] = r[128:256, :]
        dv[:, cols] = r[256:384, :]


def xor(value, axis, mask, name="exchange"):
    with jax.named_scope(name):
        return lax.ppermute(value, axis, [(s, s ^ mask) for s in range(lax.axis_size(axis))])


def own_head(z):
    return (z & 3) ^ (2 * (z >> 2))


def shards(queries, keys, values, log_decay, beta, level_weights, document_ends, out_weight, grad_y, final_state_grad):
    s = lax.axis_index("seq")
    h = lax.axis_index("head")
    z = s & 7
    where = jnp.stack([z & 3, z >> 2, s >> 3, h, own_head(z), h & 1, 0 * h, 0 * h]).astype(jnp.int32)
    packs = call(
        3, pack_body,
        [((544, 128), BF)] * 4,
        [where, document_ends, queries, keys, values, grad_y, log_decay, beta, level_weights],
        [pltpu.VMEM((SCAL, 128), F32)],
        fetch=True,
    )
    mine = [xor(packs[m], "seq", m, "reshard") for m in (1, 2, 3)]
    half = xor(out_weight, "seq", 6, "weight_half")
    w0, own = call(1, join_weight_body, [((1024, 128), BF), ((544, 128), BF)], [out_weight, half, packs[0]])
    weight = [w0] + [xor(w0, "seq", 8 * n, "weight_y") for n in (1, 2, 3)]
    mine = [own] + mine
    gm = call(1, collect_body, [((512, 128), BF)], mine, after=[w0])[0]
    T = (512, 128)
    S = (128, 128)
    ab, abf, kept = call(
        60, block_body,
        [((256, 128), BF), ((256, 128), F32), ((KEPT, 128), F32)],
        [where] + mine,
        [pltpu.VMEM((4, 288, 128), BF)],
        after=[gm],
    )
    other = xor(ab, "seq", 6, "scan_half")
    ga = [gm] + [xor(gm, "head", 2 * n, "grad_y_x") for n in (1, 2, 3)]
    gj = call(1, join_body, [((2048, 128), BF)], ga, after=[ab] + weight[1:])[0]
    gb = xor(gj, "head", 1, "grad_y_core")
    back = call(3, back_product_body, [(T, F32), (T, BF), (T, BF), (T, BF)], [where, gj, gb] + weight, [pltpu.VMEM((8, 512, 128), BF)])
    pair_bf, pair_f, omap = call(
        1, pair_body, [((256, 128), BF), ((256, 128), F32), ((256, 128), F32)], [where, abf, other], after=[back[1]]
    )
    far = [xor(pair_bf, "seq", 8 * n, "scan_y") for n in (1, 2, 3)]
    held, later = call(
        4, query_body,
        [((1536, 128), F32), ((KEPT_LATER, 128), F32)],
        [where] + mine + [kept],
        [pltpu.VMEM((4, SCAL, 128), BF), pltpu.VMEM((4,) + S, BF)],
        after=[pair_bf],
    )
    attn, far_states, ups, fin = call(
        2, far_body,
        [(T, BF), ((128, 384), F32), ((4,) + S, F32), (S, F32)],
        [where, pair_f] + far + [omap, held, final_state_grad],
        [pltpu.VMEM((4, 256, 128), F32)],
    )
    rb = [xor(back[m], "seq", m, "grad_attn") for m in (1, 2, 3)]
    do, z5, z6, x4 = call(
        2, reach_body, [((4,) + S, BF), (S, BF), (S, BF), (S, F32)], [where, back[0]] + rb + [held, omap], after=[attn]
    )
    near = [xor(z5, "seq", 8, "back_y"), xor(z6, "seq", 16, "back_y"), xor(z6, "seq", 24, "back_y")]
    send, local = call(1, near_body, [(S, BF), (S, F32)], [where] + near + [ups, abf, fin, x4])
    got = xor(send, "seq", 6, "back_half")

    at = [attn] + [xor(attn, "seq", m, "attn") for m in (1, 2, 3)]
    even, odd = call(3, project_body, [((2048, 128), BF)] * 2, [where] + at + weight, [pltpu.VMEM((8, 512, 128), BF)], after=[send])
    swapped = xor(odd, "head", 1, "out_core")
    sums = call(1, sum_pair_body, [(T, F32), (T, BF), (T, BF), (T, BF)], [even, swapped], after=[got])
    rx = [xor(sums[n], "head", 2 * n, "out_x") for n in (1, 2, 3)]
    dq, dv_part, gmap = call(
        4, grad_body,
        [((4,) + S, BF), (T, F32), (T, F32)],
        [where, do, held, far_states, kept, later],
        after=[sums[1]],
    )
    dv = call(1, value_body, [((4,) + S, BF)], [where, got, local, other, dv_part, gmap])[0]
    parts = call(
        1, sum_last_body, [((384, 128), BF)] * 4, [where, sums[0]] + rx + [dq, dv], [pltpu.VMEM((4,) + S, BF)]
    )
    home = [parts[0]] + [xor(parts[m], "seq", m, "home") for m in (1, 2, 3)]
    return tuple(call(1, place_body, [((128, 512), BF)] * 3, [where] + home))


def solution(mesh):
    in_specs = (
        P("seq", "head"),
        P("seq", "head"),
        P("seq", "head"),
        P("head", "seq"),
        P("head", "seq"),
        P(None, "head", "seq"),
        P("seq"),
        P("head", "seq"),
        P("seq", "head"),
        P("head", None, None),
    )
    out_specs = (P("seq", "head"), P("seq", "head"), P("seq", "head"))
    return jax.shard_map(shards, mesh=mesh, in_specs=in_specs, out_specs=out_specs, check_vma=False)
```

```python
import jax
import jax.numpy as jnp
from jax import lax
from jax.experimental import pallas as pl
from jax.experimental.pallas import tpu as pltpu
from jax.sharding import PartitionSpec as P

F32 = jnp.float32
BF = jnp.bfloat16
NN = (((1,), (0,)), ((), ()))
NT = (((1,), (1,)), ((), ()))
TIERS = 7
SCALE = 1e8
SCAL = 32
SOME_VMEM = 16 * 1024 * 1024
MOST_VMEM = 63_000_000


SIZES = (("a", 1024), ("a2", 512), ("a4", 256), ("s", 1536), ("m", 1024), ("w", 512), ("u", 512), ("inv", 512),
         ("er", 512), ("kt", 512), ("k", 512))
LATER = (("p", 512), ("qe", 512), ("qn", 512))
STARTS = {}


def lay(sizes):
    total = 0
    for name, rows in sizes:
        STARTS[name] = total
        total += rows
    return total


KEPT = lay(SIZES)
KEPT_LATER = lay(LATER)
READS = [(c, n) for c in range(8) for n in (1, 2, 3) if c >> (n - 1) & 1]


def at(name, index, rows=128):
    start = STARTS[name] + index * rows
    return slice(start, start + rows)


def mm(a, b, dims=NN):
    return lax.dot_general(a, b, dims, preferred_element_type=F32)


def split(x):
    hi = x.astype(BF)
    return hi, (x - hi.astype(F32)).astype(BF)


def stack(dims, a, b):
    return mm(jnp.concatenate(a, 1), jnp.concatenate(b, dims[0][1][0]), dims)


def dot3(a, b, dims=NN):
    ah, al = split(a)
    bh, bl = split(b)
    return stack(dims, [ah, al, ah], [bh, bh, bl])


def dot2(a, b, dims=NN):
    b = b.astype(BF)
    return stack(dims, split(a), [b, b])


TREE = dot3


def tn(a, b, dot):
    return dot(a.T, b)


def iotas(rows, cols):
    return (
        lax.broadcasted_iota(jnp.int32, (rows, cols), 0),
        lax.broadcasted_iota(jnp.int32, (rows, cols), 1),
    )


def call(us, body, out_shapes, ins, scratch=(), fetch=False, after=()):
    count, outs, waits = len(ins), len(out_shapes), len(after)
    big = [n for n, a in enumerate(ins) if a.dtype != jnp.int32]

    def fetching(*refs):
        held = refs[count + outs : count + outs + len(big)]
        sems = refs[count + outs + len(big)]
        own = list(refs[:count])
        copies = []
        for n, index in enumerate(big):
            copies.append(pltpu.make_async_copy(refs[index], held[n], sems.at[n]))
            own[index] = held[n]
        for copy in copies:
            copy.start()
        for copy in copies:
            copy.wait()
        body(*own, *refs[count : count + outs], *refs[count + outs + len(big) + 1 :])

    def waiting(*refs):
        (fetching if fetch else body)(*refs[:count], *refs[count + waits :])

    space = pltpu.HBM if fetch else pltpu.VMEM
    extra = [pltpu.VMEM(ins[n].shape, ins[n].dtype) for n in big] + [pltpu.SemaphoreType.DMA((len(big),))]
    with jax.named_scope(body.__name__.removesuffix("_body")):
        return pl.pallas_call(
            waiting,
            out_shape=[jax.ShapeDtypeStruct(s, d) for s, d in out_shapes],
            in_specs=[pl.BlockSpec(memory_space=pltpu.SMEM if a.dtype == jnp.int32 else space) for a in ins]
            + [pl.BlockSpec(memory_space=pl.ANY)] * waits,
            out_specs=[pl.BlockSpec(memory_space=pltpu.VMEM)] * outs,
            scratch_shapes=(extra if fetch else []) + list(scratch),
            cost_estimate=pl.CostEstimate(flops=int(us * SCALE), bytes_accessed=0, transcendentals=0),
            compiler_params=pltpu.CompilerParams(vmem_limit_bytes=MOST_VMEM if fetch else SOME_VMEM),
        )(*ins, *after)


def pack_body(wh, ends, q, k, v, gy, gate, rate, tiers, *rest):
    outs, scal = rest[:-1], rest[-1]
    own, core = wh[4], wh[5]
    lane = lax.broadcasted_iota(jnp.int32, (1, 128), 1)
    keep = jnp.where(
        lane < 64, 1.0 - ends[0].astype(F32), 1.0 - ends[1].astype(F32)
    )

    def put(row, value, parts):
        for part in range(parts):
            piece = value.astype(BF).astype(F32)
            scal[row + part : row + part + 1, :] = piece
            value = value - piece

    for m in range(4):
        j = own ^ m
        cols = pl.ds(pl.multiple_of(j * 128, 128), 128)
        gcols = pl.ds(pl.multiple_of((j ^ (2 * core)) * 128, 128), 128)
        scal[...] = jnp.zeros((SCAL, 128), F32)
        put(0, gate[pl.ds(j, 1), :], 3)
        put(3, rate[pl.ds(j, 1), :], 2)
        for tier in range(TIERS):
            put(5 + 2 * tier, tiers[tier, pl.ds(j, 1), :], 2)
        scal[19:20, :] = keep
        outs[m][0:128, :] = k[:, cols]
        outs[m][128:256, :] = v[:, cols]
        outs[m][256:288, :] = scal[...].astype(BF)
        outs[m][288:416, :] = q[:, cols]
        outs[m][416:544, :] = gy[:, gcols]


def collect_body(p0, p1, p2, p3, out):
    for m, p in enumerate((p0, p1, p2, p3)):
        out[128 * m : 128 * m + 128, :] = p[416:544, :]


def join_body(p0, p1, p2, p3, out):
    for m, p in enumerate((p0, p1, p2, p3)):
        out[512 * m : 512 * m + 512, :] = p[...]


def block_masks():
    row, col = iotas(128, 128)
    same = (row >> 6) == (col >> 6)
    return row, col, same & (row >= col), same & (row > col)


def gates(scal, lblk):
    cum3 = mm(lblk, scal, NT)
    eye = jnp.where(jnp.equal(*iotas(128, 128)), 1.0, 0.0).astype(BF)
    return cum3[:, 0:1] + cum3[:, 1:2] + cum3[:, 2:3], mm(eye, scal, NT)


def block_body(wh, a0, a1, a2, a3, ab_out, abf_out, kept, pack):
    zlo = wh[0]
    for m, a in enumerate((a0, a1, a2, a3)):
        pack[pl.ds(zlo ^ m, 1)] = a[0:288, :][None]
    row, col, causal, strict = block_masks()
    eye = row == col
    eyef = eye.astype(F32)
    lblk = causal.astype(BF)
    trans, writes = [], []
    saved = []
    for i in range(4):
        k = pack[i, 0:128, :]
        v = pack[i, 128:256, :]
        scal = pack[i, 256:288, :]
        scalf = scal.astype(F32)
        cum_col, cols = gates(scal, lblk)
        cumr = mm(scal, lblk, NT)
        cum_row = cumr[0:1] + cumr[1:2] + cumr[2:3]
        beta_col = cols[:, 3:4] + cols[:, 4:5]
        beta_row = scalf[3:4] + scalf[4:5]
        kf = k.astype(F32)
        rk_col = lax.rsqrt(jnp.sum(kf * kf, 1, keepdims=True) + 1e-6)
        rk_row = jnp.sum(jnp.where(eye, rk_col, 0.0), 0, keepdims=True)
        decay = rk_row * jnp.where(causal, jnp.exp(jnp.where(causal, cum_col - cum_row, 0.0)), 0.0)
        kept[at("er", i), :] = decay
        kept[at("k", i), :] = kf
        lower = jnp.where(strict, (beta_col * rk_col) * (decay * mm(k, k, NT)), 0.0)
        saved.append((k, v, scal, scalf, cum_col, cum_row, beta_row, kf, rk_col, rk_row, lower))
    lowers = [x[-1] for x in saved]
    invs = [eyef - jnp.where((row >> 1) == (col >> 1), lower, 0.0) for lower in lowers]
    for bit in range(1, 6):
        near = ((row >> (bit + 1)) == (col >> (bit + 1))) & ((row >> bit) != (col >> bit))
        steps = [dot3(inv, jnp.where(near, lower, 0.0)) for inv, lower in zip(invs, lowers)]
        steps = [dot3(step, inv) for step, inv in zip(steps, invs)]
        invs = [inv - step for inv, step in zip(invs, steps)]
    ws, us = [], []
    for x, inv in zip(saved, invs):
        k, v, cum_row, beta_row, rk_row = x[0], x[1], x[5], x[6], x[9]
        ws.append(dot2(inv * (beta_row * jnp.exp(cum_row) * rk_row), k))
        us.append(dot2(inv * beta_row, v))
    abs_ = []
    top = lax.broadcasted_iota(jnp.int32, (128, 256), 0) < 64
    for i, (x, inv, w, u) in enumerate(zip(saved, invs, ws, us)):
        cum_col, cum_row, kf, rk_col = x[4], x[5], x[7], x[8]
        kept[at("inv", i), :] = inv
        kept[at("w", i), :] = w
        kept[at("u", i), :] = u
        tail = jnp.exp(jnp.where(row[:, 0:1] < 64, cum_row[:, 63:64], cum_row[:, 127:128]) - cum_col) * rk_col
        kept[at("kt", i), :] = tail * kf
        rhs = jnp.concatenate([w, u], 1) * tail
        rhs = jnp.concatenate([jnp.where(top, rhs, 0.0), jnp.where(top, 0.0, rhs)], 1)
        kt = kf.T.astype(BF)
        abs_.append(stack(NN, [kt, kt], split(rhs)))
    for x, ab in zip(saved, abs_):
        scalf, cum_row = x[3], x[5]
        for b in range(2):
            keep = scalf[19:20, 64 * b : 64 * b + 1]
            last = cum_row[:, 64 * b + 63 : 64 * b + 64]
            trans.append(keep * (jnp.exp(last) * eyef - ab[:, 256 * b : 256 * b + 128]))
            writes.append(keep * ab[:, 256 * b + 128 : 256 * b + 256])

    def both(a, x, y):
        r = TREE(a, jnp.concatenate([x, y], 1))
        return r[:, 0:128], r[:, 128:256]

    for c in range(8):
        kept[at("a", c), :] = trans[c]
    t2, w2 = [], []
    for p in range(4):
        t, s = both(trans[2 * p + 1], trans[2 * p], writes[2 * p])
        t2.append(t)
        w2.append(s + writes[2 * p + 1])
        kept[at("a2", p), :] = t
    t4, w4 = [], []
    for h in range(2):
        t, s = both(t2[2 * h + 1], t2[2 * h], w2[2 * h])
        t4.append(t)
        w4.append(s + w2[2 * h + 1])
        kept[at("a4", h), :] = t
    tg, sg = both(t4[1], t4[0], w4[0])
    sg = sg + w4[1]
    ab_out[0:128, :] = tg.astype(BF)
    ab_out[128:256, :] = sg.astype(BF)
    abf_out[0:128, :] = tg
    abf_out[128:256, :] = sg
    map3, read3 = [], []
    for h in range(2):
        t, s = both(trans[4 * h + 2], t2[2 * h], w2[2 * h])
        map3.append(t)
        read3.append(s)
    maps = [eyef, trans[0], t2[0], map3[0], t4[0]]
    upper = [w4[0]]
    for inner in (trans[4], t2[2], map3[1]):
        t, s = both(inner, t4[0], w4[0])
        maps.append(t)
        upper.append(s)
    for c in range(8):
        kept[at("m", c), :] = maps[c]
    for n, (c, level) in enumerate(READS):
        if level == 1:
            state = writes[c - 1]
        elif level == 2:
            state = read3[c >> 2] if c & 1 else w2[2 * (c >> 2)]
        else:
            state = upper[c - 4]
        kept[at("s", n), :] = state


def query_body(wh, a0, a1, a2, a3, kept, held, later, scals, qs):
    for m, a in enumerate((a0, a1, a2, a3)):
        scals[pl.ds(wh[0] ^ m, 1)] = a[256:288, :][None]
        qs[pl.ds(wh[0] ^ m, 1)] = a[288:416, :][None]
    lblk = block_masks()[2].astype(BF)
    saved, pws, reads = [], [], []
    for i in range(4):
        q = qs[i]
        qf = q.astype(F32)
        cum_col, cols = gates(scals[i], lblk)
        rq_col = lax.rsqrt(jnp.sum(qf * qf, 1, keepdims=True) + 1e-6)
        scores = kept[at("er", i), :] * (rq_col * mm(q, kept[at("k", i), :].astype(BF), NT))
        later[at("p", i), :] = scores
        saved.append((qf, jnp.exp(cum_col), cols, rq_col, scores))
    for i in range(4):
        pws.append(dot2(saved[i][-1], jnp.concatenate([kept[at("w", i), :], kept[at("u", i), :]], 1)))
    for i in range(4):
        qf, exp_col, _, rq_col, _ = saved[i]
        qn = rq_col * qf
        qe = exp_col * qn - pws[i][:, 0:128]
        later[at("qe", i), :] = qe
        later[at("qn", i), :] = qn
        for c in (2 * i, 2 * i + 1):
            levels = [n for n in (1, 2, 3) if c >> (n - 1) & 1]
            rhs = jnp.concatenate(
                [kept[at("s", READS.index((c, n))), :] for n in levels] + [kept[at("m", c), :]], 1
            )
            reads.append(dot2(qe[64 * (c & 1) : 64 * (c & 1) + 64], rhs))
    for i in range(4):
        _, exp_col, cols, rq_col, _ = saved[i]
        weights = [cols[:, 5 + 2 * n : 6 + 2 * n] + cols[:, 6 + 2 * n : 7 + 2 * n] for n in range(TIERS)]
        beta_col = cols[:, 3:4] + cols[:, 4:5]
        held[i * 128 : (i + 1) * 128, :] = jnp.concatenate(
            weights + [cols[:, 19:20], rq_col, exp_col, beta_col, jnp.zeros((128, 128 - TIERS - 4), F32)], 1
        )
        for c in (2 * i, 2 * i + 1):
            rows = slice(64 * (c & 1), 64 * (c & 1) + 64)
            levels = [n for n in (1, 2, 3) if c >> (n - 1) & 1]
            out = weights[0][rows] * pws[i][rows, 128:256]
            for n, level in enumerate(levels):
                out = out + weights[level][rows] * reads[c][:, 128 * n : 128 * n + 128]
            held[1024 + 64 * c : 1024 + 64 * c + 64, :] = out
            held[512 + 64 * c : 512 + 64 * c + 64, :] = reads[c][:, 128 * len(levels) :]


def pair_body(wh, own, other, bf_out, f_out, omap_out):
    up = wh[1] == 1
    o = other[...].astype(F32)
    mine = own[...]
    low = jnp.where(up, o, mine)
    high = jnp.where(up, mine, o)
    both = dot3(high[0:128], jnp.concatenate([low[0:128], low[128:256]], 1))
    t = both[:, 0:128]
    s = both[:, 128:256] + high[128:256]
    f_out[0:128, :] = t
    f_out[128:256, :] = s
    bf_out[0:128, :] = t.astype(BF)
    bf_out[128:256, :] = s.astype(BF)
    row, col = iotas(128, 128)
    omap_out[0:128, :] = jnp.where(up, low[0:128], (row == col).astype(F32))
    omap_out[128:256, :] = jnp.where(up, low[128:256], 0.0)


def far_body(wh, own, r1, r2, r3, omap, held, final, attn_out, s_out, up_out, fin_out, order):
    y = wh[2]
    for n, r in enumerate((own, r1, r2, r3)):
        order[pl.ds(y ^ n, 1)] = r[...].astype(F32)[None]
    up_out[...] = order[:, 0:128, :]
    o = omap[0:128, :]
    b5 = order[pl.ds(y ^ 1, 1)][0][128:256]
    b01 = dot3(order[1, 0:128, :], order[0, 128:256, :]) + order[1, 128:256, :]
    b6 = jnp.where(y == 3, dot3(order[2, 0:128, :], b01), b01)
    both = dot3(o, jnp.concatenate([jnp.where((y & 1) == 1, b5, 0.0), jnp.where(y >= 2, b6, 0.0)], 1))
    states = jnp.concatenate([omap[128:256, :], both], 1)
    s_out[...] = states
    read = dot3(held[512:1024, :], states)
    out = held[1024:1536, :]
    for n in range(3):
        out = out + held[0:512, 4 + n : 5 + n] * read[:, 128 * n : 128 * n + 128]
    attn_out[...] = out.astype(BF)
    f = final[pl.ds(wh[4], 1)][0]
    for j in (3, 2, 1):
        f = jnp.where(y < j, tn(order[j, 0:128, :], f, dot3), f)
    fin_out[...] = f


def join_weight_body(p0, p1, pack, out, own):
    out[0:512, :] = p0[...]
    out[512:1024, :] = p1[...]
    own[...] = pack[...]


def order_weight(wh, parts, held):
    for n, part in enumerate(parts):
        for t in range(2):
            hb = 2 * (wh[2] ^ n) + (wh[1] ^ t)
            held[pl.ds(hb, 1)] = part[512 * t : 512 * t + 512, :][None]


def back_product_body(wh, ga, gb, w0, w1, w2, w3, own_out, o1, o2, o3, held):
    order_weight(wh, (w0, w1, w2, w3), held)
    total = None
    for n in range(4):
        for core, g in enumerate((ga, gb)):
            hb = wh[3] ^ (2 * n + core)
            w = held[pl.ds(hb, 1)][0]
            part = mm(g[512 * n : 512 * n + 512, :], w, NT)
            total = part if total is None else total + part
    acc = total
    for j in range(4):
        piece = acc[:, 128 * j : 128 * j + 128]

        for m, out in enumerate((own_out, o1, o2, o3)):

            @pl.when((wh[4] ^ m) == j)
            def _(piece=piece, out=out):
                out[...] = piece.astype(out.dtype)


def reach_body(wh, own, r1, r2, r3, held, omap, do_out, z5_out, z6_out, x4_out):
    for m in range(4):
        total = own[128 * m : 128 * m + 128, :]
        for k, r in ((1, r1), (2, r2), (3, r3)):
            total = total + r[128 * (m ^ k) : 128 * (m ^ k) + 128, :].astype(F32)
        do_out[pl.ds(wh[0] ^ m, 1)] = total.astype(BF)[None]
    do = do_out[...].reshape(512, 128).astype(F32)
    weighted = []
    for n in range(3):
        weighted.append(held[0:512, 4 + n : 5 + n] * do)
    x = tn(held[512:1024, :], jnp.concatenate(weighted, 1), dot2)
    x4_out[...] = jnp.where(wh[1] == 1, x[:, 0:128], 0.0)
    z = tn(omap[0:128, :], x[:, 128:384], dot2)
    z5_out[...] = z[:, 0:128].astype(BF)
    z6_out[...] = z[:, 128:256].astype(BF)


def grad_body(wh, do, held, far, kept, later, dq_out, dv_out, gmap_out):
    def weight(c, level):
        return held[64 * c : 64 * c + 64, level : level + 1]

    dof = do[...].reshape(512, 128).astype(F32)
    wd = [held[0:512, 4 + n : 5 + n] * dof for n in range(3)]
    carried = dot2(jnp.concatenate(wd, 1), far[...], NT)
    reach = {}
    dqe, dps, dqns, lefts = [], [], [], []
    for c in range(8):
        rows = slice(64 * (c & 1), 64 * (c & 1) + 64)
        doc = do[c >> 1, rows, :].astype(F32)
        levels = [n for n in (1, 2, 3) if c >> (n - 1) & 1]
        left = jnp.concatenate([weight(c, n) * doc for n in levels] + [carried[64 * c : 64 * c + 64]], 1)
        right = jnp.concatenate(
            [kept[at("s", READS.index((c, n))), :] for n in levels] + [kept[at("m", c), :]], 1
        )
        lefts.append(left)
        dqe.append(dot2(left, right, NT))
    for c in range(1, 8):
        levels = [n for n in (1, 2, 3) if c >> (n - 1) & 1]
        r = tn(later[at("qe", c, 64), :], lefts[c][:, 0 : 128 * len(levels)], dot2)
        for n, level in enumerate(levels):
            reach[c, level] = r[:, 128 * n : 128 * n + 128]
    dqe = [jnp.concatenate([dqe[2 * i], dqe[2 * i + 1]], 0) for i in range(4)]
    chunks = [slice(128 * i, 128 * i + 128) for i in range(4)]
    outs = [held[rows, 0:1] * do[i].astype(F32) for i, rows in enumerate(chunks)]
    for i in range(4):
        wu = jnp.concatenate([kept[at("w", i), :], kept[at("u", i), :]], 1)
        dps.append(dot2(jnp.concatenate([-dqe[i], outs[i]], 1), wu, NT) * kept[at("er", i), :])
    for i, rows in enumerate(chunks):
        dqns.append(held[rows, 9:10] * dqe[i] + dot2(dps[i], kept[at("k", i), :]))
    for i, rows in enumerate(chunks):
        q = later[at("qn", i), :]
        dq_out[i] = (held[rows, 8:9] * (dqns[i] - q * jnp.sum(q * dqns[i], 1, keepdims=True))).astype(BF)
    row, col = iotas(128, 128)
    eyef = (row == col).astype(F32)

    def tnn(name, index, y):
        return tn(kept[at(name, index), :], y, dot3)

    d4 = reach[4, 3] + tnn("a", 4, reach[5, 3]) + tnn("a2", 2, reach[6, 3] + tnn("a", 6, reach[7, 3]))
    pair = {
        3: None,
        2: reach[6, 2] + tnn("a", 6, reach[7, 2]),
        1: d4,
        0: reach[2, 2] + tnn("a", 2, reach[3, 2]) + tnn("a2", 1, d4),
    }
    a4 = kept[at("a4", 1), :]
    suf = {3: eyef, 2: kept[at("a2", 3), :], 1: a4, 0: dot3(a4, kept[at("a2", 1), :])}
    zero = jnp.zeros((128, 128), F32)
    odds = [zero if pair[i] is None else pair[i] for i in range(4)]
    pds = [tn(later[at("p", i), :], outs[i], dot3) for i in range(4)]
    evens = [
        reach[2 * i + 1, 1] if pair[i] is None else reach[2 * i + 1, 1] + tnn("a", 2 * i + 1, pair[i])
        for i in range(4)
    ]
    s_evens = [dot3(suf[i], kept[at("a", 2 * i + 1), :]) for i in range(4)]
    both = []
    for i, rows in enumerate(chunks):
        kk = held[rows, 7:8] * kept[at("kt", i), :]
        left = dot3(kk[0:64], jnp.concatenate([evens[i], s_evens[i].T], 1))
        right = dot3(kk[64:128], jnp.concatenate([odds[i], suf[i].T], 1))
        both.append(jnp.concatenate([left, right], 0))
    both = [jnp.concatenate([pd + hn[:, 0:128], hn[:, 128:256]], 1) for pd, hn in zip(pds, both)]
    both = [tn(kept[at("inv", i), :], both[i], dot3) for i in range(4)]
    for i, rows in enumerate(chunks):
        dv_out[rows, :] = held[rows, 10:11] * both[i][:, 0:128]
        gmap_out[rows, :] = held[rows, 10:11] * both[i][:, 128:256]


def near_body(wh, r1, r2, r3, ups, own, fin, x4, send_out, keep_out):
    y = wh[2]
    up = wh[1] == 1
    a = r2[...].astype(F32)
    b = r3[...].astype(F32)
    second = jnp.where(y == 0, a, b)
    third = jnp.where(y == 0, b, a)
    d01 = second + tn(ups[2], third, dot3)
    d01 = jnp.where(y == 0, tn(ups[1], d01, dot3), jnp.where(y == 1, d01, 0.0))
    part = d01 + jnp.where((y & 1) == 0, r1[...].astype(F32), 0.0)
    trans = own[0:128, :]
    full = part + fin[...]
    pulled = tn(trans, part, dot3) + x4[...]
    send_out[...] = jnp.where(up, pulled, part).astype(BF)
    keep_out[...] = full


def value_body(wh, r, kept, other, dv, gmap, out):
    up = wh[1] == 1
    got = r[...].astype(F32)
    pulled = tn(other[0:128, :].astype(F32), kept[...], dot3)
    g = got + jnp.where(up, kept[...], pulled)
    res = dv[...] + dot3(gmap[...], g)
    out[...] = res.astype(BF).reshape(4, 128, 128)


def project_body(wh, a0, a1, a2, a3, w0, w1, w2, w3, even, odd, held):
    order_weight(wh, (w0, w1, w2, w3), held)
    for n in range(8):
        total = None
        for m, a in enumerate((a0, a1, a2, a3)):
            rows = pl.ds(pl.multiple_of((wh[4] ^ m) * 128, 128), 128)
            w = held[pl.ds(wh[3] ^ n, 1), rows, :][0]
            part = mm(a[...], w)
            total = part if total is None else total + part
        out = odd if n & 1 else even
        out[512 * (n >> 1) : 512 * (n >> 1) + 512, :] = total.astype(BF)


def sum_pair_body(own, r, f_out, o2, o4, o6):
    f_out[...] = own[0:512, :].astype(F32) + r[0:512, :].astype(F32)
    for n, out in ((1, o2), (2, o4), (3, o6)):
        rows = slice(512 * n, 512 * n + 512)
        out[...] = (own[rows, :].astype(F32) + r[rows, :].astype(F32)).astype(BF)


def sum_last_body(wh, f, r2, r4, r6, dq, dv, o0, o1, o2, o3, done):
    total = f[...] + r2[...].astype(F32) + r4[...].astype(F32) + r6[...].astype(F32)
    done[...] = total.astype(BF).reshape(4, 128, 128)
    for m, out in enumerate((o0, o1, o2, o3)):
        for n, part in enumerate((done, dq, dv)):
            out[128 * n : 128 * n + 128, :] = part[pl.ds(wh[0] ^ m, 1)][0]


def place_body(wh, r0, r1, r2, r3, layer, dq, dv):
    for m, r in enumerate((r0, r1, r2, r3)):
        j = wh[4] ^ m
        cols = pl.ds(pl.multiple_of(j * 128, 128), 128)
        layer[:, pl.ds(pl.multiple_of((j ^ (2 * wh[5])) * 128, 128), 128)] = r[0:128, :]
        dq[:, cols] = r[128:256, :]
        dv[:, cols] = r[256:384, :]


def xor(value, axis, mask, name="exchange"):
    with jax.named_scope(name):
        return lax.ppermute(value, axis, [(s, s ^ mask) for s in range(lax.axis_size(axis))])


def own_head(z):
    return (z & 3) ^ (2 * (z >> 2))


def shards(queries, keys, values, log_decay, beta, level_weights, document_ends, out_weight, grad_y, final_state_grad):
    s = lax.axis_index("seq")
    h = lax.axis_index("head")
    z = s & 7
    where = jnp.stack([z & 3, z >> 2, s >> 3, h, own_head(z), h & 1, 0 * h, 0 * h]).astype(jnp.int32)
    packs = call(
        3, pack_body,
        [((544, 128), BF)] * 4,
        [where, document_ends, queries, keys, values, grad_y, log_decay, beta, level_weights],
        [pltpu.VMEM((SCAL, 128), F32)],
        fetch=True,
    )
    mine = [xor(packs[m], "seq", m, "reshard") for m in (1, 2, 3)]
    half = xor(out_weight, "seq", 6, "weight_half")
    w0, own = call(1, join_weight_body, [((1024, 128), BF), ((544, 128), BF)], [out_weight, half, packs[0]])
    weight = [w0] + [xor(w0, "seq", 8 * n, "weight_y") for n in (1, 2, 3)]
    mine = [own] + mine
    gm = call(1, collect_body, [((512, 128), BF)], mine, after=[w0])[0]
    T = (512, 128)
    S = (128, 128)
    ab, abf, kept = call(
        60, block_body,
        [((256, 128), BF), ((256, 128), F32), ((KEPT, 128), F32)],
        [where] + mine,
        [pltpu.VMEM((4, 288, 128), BF)],
        after=[gm],
    )
    other = xor(ab, "seq", 6, "scan_half")
    ga = [gm] + [xor(gm, "head", 2 * n, "grad_y_x") for n in (1, 2, 3)]
    gj = call(1, join_body, [((2048, 128), BF)], ga, after=[ab] + weight[1:])[0]
    gb = xor(gj, "head", 1, "grad_y_core")
    back = call(3, back_product_body, [(T, F32), (T, BF), (T, BF), (T, BF)], [where, gj, gb] + weight, [pltpu.VMEM((8, 512, 128), BF)])
    pair_bf, pair_f, omap = call(
        1, pair_body, [((256, 128), BF), ((256, 128), F32), ((256, 128), F32)], [where, abf, other], after=[back[1]]
    )
    far = [xor(pair_bf, "seq", 8 * n, "scan_y") for n in (1, 2, 3)]
    held, later = call(
        4, query_body,
        [((1536, 128), F32), ((KEPT_LATER, 128), F32)],
        [where] + mine + [kept],
        [pltpu.VMEM((4, SCAL, 128), BF), pltpu.VMEM((4,) + S, BF)],
        after=[pair_bf],
    )
    attn, far_states, ups, fin = call(
        2, far_body,
        [(T, BF), ((128, 384), F32), ((4,) + S, F32), (S, F32)],
        [where, pair_f] + far + [omap, held, final_state_grad],
        [pltpu.VMEM((4, 256, 128), F32)],
    )
    rb = [xor(back[m], "seq", m, "grad_attn") for m in (1, 2, 3)]
    do, z5, z6, x4 = call(
        2, reach_body, [((4,) + S, BF), (S, BF), (S, BF), (S, F32)], [where, back[0]] + rb + [held, omap], after=[attn]
    )
    near = [xor(z5, "seq", 8, "back_y"), xor(z6, "seq", 16, "back_y"), xor(z6, "seq", 24, "back_y")]
    send, local = call(1, near_body, [(S, BF), (S, F32)], [where] + near + [ups, abf, fin, x4])
    got = xor(send, "seq", 6, "back_half")

    at = [attn] + [xor(attn, "seq", m, "attn") for m in (1, 2, 3)]
    even, odd = call(3, project_body, [((2048, 128), BF)] * 2, [where] + at + weight, [pltpu.VMEM((8, 512, 128), BF)], after=[send])
    swapped = xor(odd, "head", 1, "out_core")
    sums = call(1, sum_pair_body, [(T, F32), (T, BF), (T, BF), (T, BF)], [even, swapped])
    rx = [xor(sums[n], "head", 2 * n, "out_x") for n in (1, 2, 3)]
    dq, dv_part, gmap = call(
        200, grad_body,
        [((4,) + S, BF), (T, F32), (T, F32)],
        [where, do, held, far_states, kept, later],
        after=[got],
    )
    dv = call(1, value_body, [((4,) + S, BF)], [where, got, local, other, dv_part, gmap])[0]
    parts = call(
        1, sum_last_body, [((384, 128), BF)] * 4, [where, sums[0]] + rx + [dq, dv], [pltpu.VMEM((4,) + S, BF)]
    )
    home = [parts[0]] + [xor(parts[m], "seq", m, "home") for m in (1, 2, 3)]
    return tuple(call(1, place_body, [((128, 512), BF)] * 3, [where] + home))


def solution(mesh):
    in_specs = (
        P("seq", "head"),
        P("seq", "head"),
        P("seq", "head"),
        P("head", "seq"),
        P("head", "seq"),
        P(None, "head", "seq"),
        P("seq"),
        P("head", "seq"),
        P("seq", "head"),
        P("head", None, None),
    )
    out_specs = (P("seq", "head"), P("seq", "head"), P("seq", "head"))
    return jax.shard_map(shards, mesh=mesh, in_specs=in_specs, out_specs=out_specs, check_vma=False)
```

```python
import jax
import jax.numpy as jnp
from jax import lax
from jax.experimental import pallas as pl
from jax.experimental.pallas import tpu as pltpu
from jax.sharding import PartitionSpec as P

F32 = jnp.float32
BF = jnp.bfloat16
NN = (((1,), (0,)), ((), ()))
NT = (((1,), (1,)), ((), ()))
TIERS = 7
SCALE = 1e8
SCAL = 32
SOME_VMEM = 16 * 1024 * 1024
MOST_VMEM = 63_000_000


SIZES = (("a", 1024), ("a2", 512), ("a4", 256), ("s", 1536), ("m", 1024), ("w", 512), ("u", 512), ("inv", 512),
         ("er", 512), ("kt", 512), ("k", 512))
LATER = (("p", 512), ("qe", 512), ("qn", 512))
STARTS = {}


def lay(sizes):
    total = 0
    for name, rows in sizes:
        STARTS[name] = total
        total += rows
    return total


KEPT = lay(SIZES)
KEPT_LATER = lay(LATER)
READS = [(c, n) for c in range(8) for n in (1, 2, 3) if c >> (n - 1) & 1]


def at(name, index, rows=128):
    start = STARTS[name] + index * rows
    return slice(start, start + rows)


def mm(a, b, dims=NN):
    return lax.dot_general(a, b, dims, preferred_element_type=F32)


def split(x):
    hi = x.astype(BF)
    return hi, (x - hi.astype(F32)).astype(BF)


def stack(dims, a, b):
    return mm(jnp.concatenate(a, 1), jnp.concatenate(b, dims[0][1][0]), dims)


def dot3(a, b, dims=NN):
    ah, al = split(a)
    bh, bl = split(b)
    return stack(dims, [ah, al, ah], [bh, bh, bl])


def dot2(a, b, dims=NN):
    b = b.astype(BF)
    return stack(dims, split(a), [b, b])


TREE = dot3


def tn(a, b, dot):
    return dot(a.T, b)


def iotas(rows, cols):
    return (
        lax.broadcasted_iota(jnp.int32, (rows, cols), 0),
        lax.broadcasted_iota(jnp.int32, (rows, cols), 1),
    )


def call(us, body, out_shapes, ins, scratch=(), fetch=False, after=()):
    count, outs, waits = len(ins), len(out_shapes), len(after)
    big = [n for n, a in enumerate(ins) if a.dtype != jnp.int32]

    def fetching(*refs):
        held = refs[count + outs : count + outs + len(big)]
        sems = refs[count + outs + len(big)]
        own = list(refs[:count])
        copies = []
        for n, index in enumerate(big):
            copies.append(pltpu.make_async_copy(refs[index], held[n], sems.at[n]))
            own[index] = held[n]
        for copy in copies:
            copy.start()
        for copy in copies:
            copy.wait()
        body(*own, *refs[count : count + outs], *refs[count + outs + len(big) + 1 :])

    def waiting(*refs):
        (fetching if fetch else body)(*refs[:count], *refs[count + waits :])

    space = pltpu.HBM if fetch else pltpu.VMEM
    extra = [pltpu.VMEM(ins[n].shape, ins[n].dtype) for n in big] + [pltpu.SemaphoreType.DMA((len(big),))]
    with jax.named_scope(body.__name__.removesuffix("_body")):
        return pl.pallas_call(
            waiting,
            out_shape=[jax.ShapeDtypeStruct(s, d) for s, d in out_shapes],
            in_specs=[pl.BlockSpec(memory_space=pltpu.SMEM if a.dtype == jnp.int32 else space) for a in ins]
            + [pl.BlockSpec(memory_space=pl.ANY)] * waits,
            out_specs=[pl.BlockSpec(memory_space=pltpu.VMEM)] * outs,
            scratch_shapes=(extra if fetch else []) + list(scratch),
            cost_estimate=pl.CostEstimate(flops=int(us * SCALE), bytes_accessed=0, transcendentals=0),
            compiler_params=pltpu.CompilerParams(vmem_limit_bytes=MOST_VMEM if fetch else SOME_VMEM),
        )(*ins, *after)


def pack_body(wh, ends, q, k, v, gy, gate, rate, tiers, *rest):
    outs, scal = rest[:-1], rest[-1]
    own, core = wh[4], wh[5]
    lane = lax.broadcasted_iota(jnp.int32, (1, 128), 1)
    keep = jnp.where(
        lane < 64, 1.0 - ends[0].astype(F32), 1.0 - ends[1].astype(F32)
    )

    def put(row, value, parts):
        for part in range(parts):
            piece = value.astype(BF).astype(F32)
            scal[row + part : row + part + 1, :] = piece
            value = value - piece

    for m in range(4):
        j = own ^ m
        cols = pl.ds(pl.multiple_of(j * 128, 128), 128)
        gcols = pl.ds(pl.multiple_of((j ^ (2 * core)) * 128, 128), 128)
        scal[...] = jnp.zeros((SCAL, 128), F32)
        put(0, gate[pl.ds(j, 1), :], 3)
        put(3, rate[pl.ds(j, 1), :], 2)
        for tier in range(TIERS):
            put(5 + 2 * tier, tiers[tier, pl.ds(j, 1), :], 2)
        scal[19:20, :] = keep
        outs[m][0:128, :] = k[:, cols]
        outs[m][128:256, :] = v[:, cols]
        outs[m][256:288, :] = scal[...].astype(BF)
        outs[m][288:416, :] = q[:, cols]
        outs[m][416:544, :] = gy[:, gcols]


def collect_body(p0, p1, p2, p3, out):
    for m, p in enumerate((p0, p1, p2, p3)):
        out[128 * m : 128 * m + 128, :] = p[416:544, :]


def join_body(p0, p1, p2, p3, out):
    for m, p in enumerate((p0, p1, p2, p3)):
        out[512 * m : 512 * m + 512, :] = p[...]


def block_masks():
    row, col = iotas(128, 128)
    same = (row >> 6) == (col >> 6)
    return row, col, same & (row >= col), same & (row > col)


def gates(scal, lblk):
    cum3 = mm(lblk, scal, NT)
    eye = jnp.where(jnp.equal(*iotas(128, 128)), 1.0, 0.0).astype(BF)
    return cum3[:, 0:1] + cum3[:, 1:2] + cum3[:, 2:3], mm(eye, scal, NT)


def block_body(wh, a0, a1, a2, a3, ab_out, abf_out, kept, pack):
    zlo = wh[0]
    for m, a in enumerate((a0, a1, a2, a3)):
        pack[pl.ds(zlo ^ m, 1)] = a[0:288, :][None]
    row, col, causal, strict = block_masks()
    eye = row == col
    eyef = eye.astype(F32)
    lblk = causal.astype(BF)
    trans, writes = [], []
    saved = []
    for i in range(4):
        k = pack[i, 0:128, :]
        v = pack[i, 128:256, :]
        scal = pack[i, 256:288, :]
        scalf = scal.astype(F32)
        cum_col, cols = gates(scal, lblk)
        cumr = mm(scal, lblk, NT)
        cum_row = cumr[0:1] + cumr[1:2] + cumr[2:3]
        beta_col = cols[:, 3:4] + cols[:, 4:5]
        beta_row = scalf[3:4] + scalf[4:5]
        kf = k.astype(F32)
        rk_col = lax.rsqrt(jnp.sum(kf * kf, 1, keepdims=True) + 1e-6)
        rk_row = jnp.sum(jnp.where(eye, rk_col, 0.0), 0, keepdims=True)
        decay = rk_row * jnp.where(causal, jnp.exp(jnp.where(causal, cum_col - cum_row, 0.0)), 0.0)
        kept[at("er", i), :] = decay
        kept[at("k", i), :] = kf
        lower = jnp.where(strict, (beta_col * rk_col) * (decay * mm(k, k, NT)), 0.0)
        saved.append((k, v, scal, scalf, cum_col, cum_row, beta_row, kf, rk_col, rk_row, lower))
    lowers = [x[-1] for x in saved]
    invs = [eyef - jnp.where((row >> 1) == (col >> 1), lower, 0.0) for lower in lowers]
    for bit in range(1, 6):
        near = ((row >> (bit + 1)) == (col >> (bit + 1))) & ((row >> bit) != (col >> bit))
        steps = [dot3(inv, jnp.where(near, lower, 0.0)) for inv, lower in zip(invs, lowers)]
        steps = [dot3(step, inv) for step, inv in zip(steps, invs)]
        invs = [inv - step for inv, step in zip(invs, steps)]
    ws, us = [], []
    for x, inv in zip(saved, invs):
        k, v, cum_row, beta_row, rk_row = x[0], x[1], x[5], x[6], x[9]
        ws.append(dot2(inv * (beta_row * jnp.exp(cum_row) * rk_row), k))
        us.append(dot2(inv * beta_row, v))
    abs_ = []
    top = lax.broadcasted_iota(jnp.int32, (128, 256), 0) < 64
    for i, (x, inv, w, u) in enumerate(zip(saved, invs, ws, us)):
        cum_col, cum_row, kf, rk_col = x[4], x[5], x[7], x[8]
        kept[at("inv", i), :] = inv
        kept[at("w", i), :] = w
        kept[at("u", i), :] = u
        tail = jnp.exp(jnp.where(row[:, 0:1] < 64, cum_row[:, 63:64], cum_row[:, 127:128]) - cum_col) * rk_col
        kept[at("kt", i), :] = tail * kf
        rhs = jnp.concatenate([w, u], 1) * tail
        rhs = jnp.concatenate([jnp.where(top, rhs, 0.0), jnp.where(top, 0.0, rhs)], 1)
        kt = kf.T.astype(BF)
        abs_.append(stack(NN, [kt, kt], split(rhs)))
    for x, ab in zip(saved, abs_):
        scalf, cum_row = x[3], x[5]
        for b in range(2):
            keep = scalf[19:20, 64 * b : 64 * b + 1]
            last = cum_row[:, 64 * b + 63 : 64 * b + 64]
            trans.append(keep * (jnp.exp(last) * eyef - ab[:, 256 * b : 256 * b + 128]))
            writes.append(keep * ab[:, 256 * b + 128 : 256 * b + 256])

    def both(a, x, y):
        r = TREE(a, jnp.concatenate([x, y], 1))
        return r[:, 0:128], r[:, 128:256]

    for c in range(8):
        kept[at("a", c), :] = trans[c]
    t2, w2 = [], []
    for p in range(4):
        t, s = both(trans[2 * p + 1], trans[2 * p], writes[2 * p])
        t2.append(t)
        w2.append(s + writes[2 * p + 1])
        kept[at("a2", p), :] = t
    t4, w4 = [], []
    for h in range(2):
        t, s = both(t2[2 * h + 1], t2[2 * h], w2[2 * h])
        t4.append(t)
        w4.append(s + w2[2 * h + 1])
        kept[at("a4", h), :] = t
    tg, sg = both(t4[1], t4[0], w4[0])
    sg = sg + w4[1]
    ab_out[0:128, :] = tg.astype(BF)
    ab_out[128:256, :] = sg.astype(BF)
    abf_out[0:128, :] = tg
    abf_out[128:256, :] = sg
    map3, read3 = [], []
    for h in range(2):
        t, s = both(trans[4 * h + 2], t2[2 * h], w2[2 * h])
        map3.append(t)
        read3.append(s)
    maps = [eyef, trans[0], t2[0], map3[0], t4[0]]
    upper = [w4[0]]
    for inner in (trans[4], t2[2], map3[1]):
        t, s = both(inner, t4[0], w4[0])
        maps.append(t)
        upper.append(s)
    for c in range(8):
        kept[at("m", c), :] = maps[c]
    for n, (c, level) in enumerate(READS):
        if level == 1:
            state = writes[c - 1]
        elif level == 2:
            state = read3[c >> 2] if c & 1 else w2[2 * (c >> 2)]
        else:
            state = upper[c - 4]
        kept[at("s", n), :] = state


def query_body(wh, a0, a1, a2, a3, kept, held, later, scals, qs):
    for m, a in enumerate((a0, a1, a2, a3)):
        scals[pl.ds(wh[0] ^ m, 1)] = a[256:288, :][None]
        qs[pl.ds(wh[0] ^ m, 1)] = a[288:416, :][None]
    lblk = block_masks()[2].astype(BF)
    saved, pws, reads = [], [], []
    for i in range(4):
        q = qs[i]
        qf = q.astype(F32)
        cum_col, cols = gates(scals[i], lblk)
        rq_col = lax.rsqrt(jnp.sum(qf * qf, 1, keepdims=True) + 1e-6)
        scores = kept[at("er", i), :] * (rq_col * mm(q, kept[at("k", i), :].astype(BF), NT))
        later[at("p", i), :] = scores
        saved.append((qf, jnp.exp(cum_col), cols, rq_col, scores))
    for i in range(4):
        pws.append(dot2(saved[i][-1], jnp.concatenate([kept[at("w", i), :], kept[at("u", i), :]], 1)))
    for i in range(4):
        qf, exp_col, _, rq_col, _ = saved[i]
        qn = rq_col * qf
        qe = exp_col * qn - pws[i][:, 0:128]
        later[at("qe", i), :] = qe
        later[at("qn", i), :] = qn
        for c in (2 * i, 2 * i + 1):
            levels = [n for n in (1, 2, 3) if c >> (n - 1) & 1]
            rhs = jnp.concatenate(
                [kept[at("s", READS.index((c, n))), :] for n in levels] + [kept[at("m", c), :]], 1
            )
            reads.append(dot2(qe[64 * (c & 1) : 64 * (c & 1) + 64], rhs))
    for i in range(4):
        _, exp_col, cols, rq_col, _ = saved[i]
        weights = [cols[:, 5 + 2 * n : 6 + 2 * n] + cols[:, 6 + 2 * n : 7 + 2 * n] for n in range(TIERS)]
        beta_col = cols[:, 3:4] + cols[:, 4:5]
        held[i * 128 : (i + 1) * 128, :] = jnp.concatenate(
            weights + [cols[:, 19:20], rq_col, exp_col, beta_col, jnp.zeros((128, 128 - TIERS - 4), F32)], 1
        )
        for c in (2 * i, 2 * i + 1):
            rows = slice(64 * (c & 1), 64 * (c & 1) + 64)
            levels = [n for n in (1, 2, 3) if c >> (n - 1) & 1]
            out = weights[0][rows] * pws[i][rows, 128:256]
            for n, level in enumerate(levels):
                out = out + weights[level][rows] * reads[c][:, 128 * n : 128 * n + 128]
            held[1024 + 64 * c : 1024 + 64 * c + 64, :] = out
            held[512 + 64 * c : 512 + 64 * c + 64, :] = reads[c][:, 128 * len(levels) :]


def pair_body(wh, own, other, bf_out, f_out, omap_out):
    up = wh[1] == 1
    o = other[...].astype(F32)
    mine = own[...]
    low = jnp.where(up, o, mine)
    high = jnp.where(up, mine, o)
    both = dot3(high[0:128], jnp.concatenate([low[0:128], low[128:256]], 1))
    t = both[:, 0:128]
    s = both[:, 128:256] + high[128:256]
    f_out[0:128, :] = t
    f_out[128:256, :] = s
    bf_out[0:128, :] = t.astype(BF)
    bf_out[128:256, :] = s.astype(BF)
    row, col = iotas(128, 128)
    omap_out[0:128, :] = jnp.where(up, low[0:128], (row == col).astype(F32))
    omap_out[128:256, :] = jnp.where(up, low[128:256], 0.0)


def far_body(wh, own, r1, r2, r3, omap, held, final, attn_out, s_out, up_out, fin_out, order):
    y = wh[2]
    for n, r in enumerate((own, r1, r2, r3)):
        order[pl.ds(y ^ n, 1)] = r[...].astype(F32)[None]
    up_out[...] = order[:, 0:128, :]
    o = omap[0:128, :]
    b5 = order[pl.ds(y ^ 1, 1)][0][128:256]
    b01 = dot3(order[1, 0:128, :], order[0, 128:256, :]) + order[1, 128:256, :]
    b6 = jnp.where(y == 3, dot3(order[2, 0:128, :], b01), b01)
    both = dot3(o, jnp.concatenate([jnp.where((y & 1) == 1, b5, 0.0), jnp.where(y >= 2, b6, 0.0)], 1))
    states = jnp.concatenate([omap[128:256, :], both], 1)
    s_out[...] = states
    read = dot3(held[512:1024, :], states)
    out = held[1024:1536, :]
    for n in range(3):
        out = out + held[0:512, 4 + n : 5 + n] * read[:, 128 * n : 128 * n + 128]
    attn_out[...] = out.astype(BF)
    f = final[pl.ds(wh[4], 1)][0]
    for j in (3, 2, 1):
        f = jnp.where(y < j, tn(order[j, 0:128, :], f, dot3), f)
    fin_out[...] = f


def join_weight_body(p0, p1, pack, out, own):
    out[0:512, :] = p0[...]
    out[512:1024, :] = p1[...]
    own[...] = pack[...]


def order_weight(wh, parts, held):
    for n, part in enumerate(parts):
        for t in range(2):
            hb = 2 * (wh[2] ^ n) + (wh[1] ^ t)
            held[pl.ds(hb, 1)] = part[512 * t : 512 * t + 512, :][None]


def back_product_body(wh, ga, gb, w0, w1, w2, w3, own_out, o1, o2, o3, held):
    order_weight(wh, (w0, w1, w2, w3), held)
    total = None
    for n in range(4):
        for core, g in enumerate((ga, gb)):
            hb = wh[3] ^ (2 * n + core)
            w = held[pl.ds(hb, 1)][0]
            part = mm(g[512 * n : 512 * n + 512, :], w, NT)
            total = part if total is None else total + part
    acc = total
    for j in range(4):
        piece = acc[:, 128 * j : 128 * j + 128]

        for m, out in enumerate((own_out, o1, o2, o3)):

            @pl.when((wh[4] ^ m) == j)
            def _(piece=piece, out=out):
                out[...] = piece.astype(out.dtype)


def reach_body(wh, own, r1, r2, r3, held, omap, do_out, z5_out, z6_out, x4_out):
    for m in range(4):
        total = own[128 * m : 128 * m + 128, :]
        for k, r in ((1, r1), (2, r2), (3, r3)):
            total = total + r[128 * (m ^ k) : 128 * (m ^ k) + 128, :].astype(F32)
        do_out[pl.ds(wh[0] ^ m, 1)] = total.astype(BF)[None]
    do = do_out[...].reshape(512, 128).astype(F32)
    weighted = []
    for n in range(3):
        weighted.append(held[0:512, 4 + n : 5 + n] * do)
    x = tn(held[512:1024, :], jnp.concatenate(weighted, 1), dot2)
    x4_out[...] = jnp.where(wh[1] == 1, x[:, 0:128], 0.0)
    z = tn(omap[0:128, :], x[:, 128:384], dot2)
    z5_out[...] = z[:, 0:128].astype(BF)
    z6_out[...] = z[:, 128:256].astype(BF)


def grad_body(wh, do, held, far, kept, later, dq_out, dv_out, gmap_out):
    def weight(c, level):
        return held[64 * c : 64 * c + 64, level : level + 1]

    dof = do[...].reshape(512, 128).astype(F32)
    wd = [held[0:512, 4 + n : 5 + n] * dof for n in range(3)]
    carried = dot2(jnp.concatenate(wd, 1), far[...], NT)
    reach = {}
    dqe, dps, dqns, lefts = [], [], [], []
    for c in range(8):
        rows = slice(64 * (c & 1), 64 * (c & 1) + 64)
        doc = do[c >> 1, rows, :].astype(F32)
        levels = [n for n in (1, 2, 3) if c >> (n - 1) & 1]
        left = jnp.concatenate([weight(c, n) * doc for n in levels] + [carried[64 * c : 64 * c + 64]], 1)
        right = jnp.concatenate(
            [kept[at("s", READS.index((c, n))), :] for n in levels] + [kept[at("m", c), :]], 1
        )
        lefts.append(left)
        dqe.append(dot2(left, right, NT))
    for c in range(1, 8):
        levels = [n for n in (1, 2, 3) if c >> (n - 1) & 1]
        r = tn(later[at("qe", c, 64), :], lefts[c][:, 0 : 128 * len(levels)], dot2)
        for n, level in enumerate(levels):
            reach[c, level] = r[:, 128 * n : 128 * n + 128]
    dqe = [jnp.concatenate([dqe[2 * i], dqe[2 * i + 1]], 0) for i in range(4)]
    chunks = [slice(128 * i, 128 * i + 128) for i in range(4)]
    outs = [held[rows, 0:1] * do[i].astype(F32) for i, rows in enumerate(chunks)]
    for i in range(4):
        wu = jnp.concatenate([kept[at("w", i), :], kept[at("u", i), :]], 1)
        dps.append(dot2(jnp.concatenate([-dqe[i], outs[i]], 1), wu, NT) * kept[at("er", i), :])
    for i, rows in enumerate(chunks):
        dqns.append(held[rows, 9:10] * dqe[i] + dot2(dps[i], kept[at("k", i), :]))
    for i, rows in enumerate(chunks):
        q = later[at("qn", i), :]
        dq_out[i] = (held[rows, 8:9] * (dqns[i] - q * jnp.sum(q * dqns[i], 1, keepdims=True))).astype(BF)
    row, col = iotas(128, 128)
    eyef = (row == col).astype(F32)

    def tnn(name, index, y):
        return tn(kept[at(name, index), :], y, dot3)

    d4 = reach[4, 3] + tnn("a", 4, reach[5, 3]) + tnn("a2", 2, reach[6, 3] + tnn("a", 6, reach[7, 3]))
    pair = {
        3: None,
        2: reach[6, 2] + tnn("a", 6, reach[7, 2]),
        1: d4,
        0: reach[2, 2] + tnn("a", 2, reach[3, 2]) + tnn("a2", 1, d4),
    }
    a4 = kept[at("a4", 1), :]
    suf = {3: eyef, 2: kept[at("a2", 3), :], 1: a4, 0: dot3(a4, kept[at("a2", 1), :])}
    zero = jnp.zeros((128, 128), F32)
    odds = [zero if pair[i] is None else pair[i] for i in range(4)]
    pds = [tn(later[at("p", i), :], outs[i], dot3) for i in range(4)]
    evens = [
        reach[2 * i + 1, 1] if pair[i] is None else reach[2 * i + 1, 1] + tnn("a", 2 * i + 1, pair[i])
        for i in range(4)
    ]
    s_evens = [dot3(suf[i], kept[at("a", 2 * i + 1), :]) for i in range(4)]
    both = []
    for i, rows in enumerate(chunks):
        kk = held[rows, 7:8] * kept[at("kt", i), :]
        left = dot3(kk[0:64], jnp.concatenate([evens[i], s_evens[i].T], 1))
        right = dot3(kk[64:128], jnp.concatenate([odds[i], suf[i].T], 1))
        both.append(jnp.concatenate([left, right], 0))
    both = [jnp.concatenate([pd + hn[:, 0:128], hn[:, 128:256]], 1) for pd, hn in zip(pds, both)]
    both = [tn(kept[at("inv", i), :], both[i], dot3) for i in range(4)]
    for i, rows in enumerate(chunks):
        dv_out[rows, :] = held[rows, 10:11] * both[i][:, 0:128]
        gmap_out[rows, :] = held[rows, 10:11] * both[i][:, 128:256]


def near_body(wh, r1, r2, r3, ups, own, fin, x4, send_out, keep_out):
    y = wh[2]
    up = wh[1] == 1
    a = r2[...].astype(F32)
    b = r3[...].astype(F32)
    second = jnp.where(y == 0, a, b)
    third = jnp.where(y == 0, b, a)
    d01 = second + tn(ups[2], third, dot3)
    d01 = jnp.where(y == 0, tn(ups[1], d01, dot3), jnp.where(y == 1, d01, 0.0))
    part = d01 + jnp.where((y & 1) == 0, r1[...].astype(F32), 0.0)
    trans = own[0:128, :]
    full = part + fin[...]
    pulled = tn(trans, part, dot3) + x4[...]
    send_out[...] = jnp.where(up, pulled, part).astype(BF)
    keep_out[...] = full


def value_body(wh, r, kept, other, dv, gmap, out):
    up = wh[1] == 1
    got = r[...].astype(F32)
    pulled = tn(other[0:128, :].astype(F32), kept[...], dot3)
    g = got + jnp.where(up, kept[...], pulled)
    res = dv[...] + dot3(gmap[...], g)
    out[...] = res.astype(BF).reshape(4, 128, 128)


def project_body(wh, a0, a1, a2, a3, w0, w1, w2, w3, even, odd, held):
    order_weight(wh, (w0, w1, w2, w3), held)
    for n in range(8):
        total = None
        for m, a in enumerate((a0, a1, a2, a3)):
            rows = pl.ds(pl.multiple_of((wh[4] ^ m) * 128, 128), 128)
            w = held[pl.ds(wh[3] ^ n, 1), rows, :][0]
            part = mm(a[...], w)
            total = part if total is None else total + part
        out = odd if n & 1 else even
        out[512 * (n >> 1) : 512 * (n >> 1) + 512, :] = total.astype(BF)


def sum_pair_body(own, r, f_out, o2, o4, o6):
    f_out[...] = own[0:512, :].astype(F32) + r[0:512, :].astype(F32)
    for n, out in ((1, o2), (2, o4), (3, o6)):
        rows = slice(512 * n, 512 * n + 512)
        out[...] = (own[rows, :].astype(F32) + r[rows, :].astype(F32)).astype(BF)


def sum_last_body(wh, f, r2, r4, r6, dq, dv, o0, o1, o2, o3, done):
    total = f[...] + r2[...].astype(F32) + r4[...].astype(F32) + r6[...].astype(F32)
    done[...] = total.astype(BF).reshape(4, 128, 128)
    for m, out in enumerate((o0, o1, o2, o3)):
        for n, part in enumerate((done, dq, dv)):
            out[128 * n : 128 * n + 128, :] = part[pl.ds(wh[0] ^ m, 1)][0]


def place_body(wh, r0, r1, r2, r3, layer, dq, dv):
    for m, r in enumerate((r0, r1, r2, r3)):
        j = wh[4] ^ m
        cols = pl.ds(pl.multiple_of(j * 128, 128), 128)
        layer[:, pl.ds(pl.multiple_of((j ^ (2 * wh[5])) * 128, 128), 128)] = r[0:128, :]
        dq[:, cols] = r[128:256, :]
        dv[:, cols] = r[256:384, :]


def xor(value, axis, mask, name="exchange"):
    with jax.named_scope(name):
        return lax.ppermute(value, axis, [(s, s ^ mask) for s in range(lax.axis_size(axis))])


def own_head(z):
    return (z & 3) ^ (2 * (z >> 2))


def shards(queries, keys, values, log_decay, beta, level_weights, document_ends, out_weight, grad_y, final_state_grad):
    s = lax.axis_index("seq")
    h = lax.axis_index("head")
    z = s & 7
    where = jnp.stack([z & 3, z >> 2, s >> 3, h, own_head(z), h & 1, 0 * h, 0 * h]).astype(jnp.int32)
    packs = call(
        3, pack_body,
        [((544, 128), BF)] * 4,
        [where, document_ends, queries, keys, values, grad_y, log_decay, beta, level_weights],
        [pltpu.VMEM((SCAL, 128), F32)],
        fetch=True,
    )
    mine = [xor(packs[m], "seq", m, "reshard") for m in (1, 2, 3)]
    half = xor(out_weight, "seq", 6, "weight_half")
    w0, own = call(1, join_weight_body, [((1024, 128), BF), ((544, 128), BF)], [out_weight, half, packs[0]])
    weight = [w0] + [xor(w0, "seq", 8 * n, "weight_y") for n in (1, 2, 3)]
    mine = [own] + mine
    gm = call(200, collect_body, [((512, 128), BF)], mine, after=[w0])[0]
    T = (512, 128)
    S = (128, 128)
    ab, abf, kept = call(
        60, block_body,
        [((256, 128), BF), ((256, 128), F32), ((KEPT, 128), F32)],
        [where] + mine,
        [pltpu.VMEM((4, 288, 128), BF)],
        after=[gm, weight[1]],
    )
    other = xor(ab, "seq", 6, "scan_half")
    ga = [gm] + [xor(gm, "head", 2 * n, "grad_y_x") for n in (1, 2, 3)]
    gj = call(1, join_body, [((2048, 128), BF)], ga, after=[ab] + weight[1:])[0]
    gb = xor(gj, "head", 1, "grad_y_core")
    back = call(3, back_product_body, [(T, F32), (T, BF), (T, BF), (T, BF)], [where, gj, gb] + weight, [pltpu.VMEM((8, 512, 128), BF)])
    pair_bf, pair_f, omap = call(
        1, pair_body, [((256, 128), BF), ((256, 128), F32), ((256, 128), F32)], [where, abf, other], after=[back[1]]
    )
    far = [xor(pair_bf, "seq", 8 * n, "scan_y") for n in (1, 2, 3)]
    held, later = call(
        4, query_body,
        [((1536, 128), F32), ((KEPT_LATER, 128), F32)],
        [where] + mine + [kept],
        [pltpu.VMEM((4, SCAL, 128), BF), pltpu.VMEM((4,) + S, BF)],
        after=[pair_bf],
    )
    attn, far_states, ups, fin = call(
        2, far_body,
        [(T, BF), ((128, 384), F32), ((4,) + S, F32), (S, F32)],
        [where, pair_f] + far + [omap, held, final_state_grad],
        [pltpu.VMEM((4, 256, 128), F32)],
    )
    rb = [xor(back[m], "seq", m, "grad_attn") for m in (1, 2, 3)]
    do, z5, z6, x4 = call(
        2, reach_body, [((4,) + S, BF), (S, BF), (S, BF), (S, F32)], [where, back[0]] + rb + [held, omap], after=[attn]
    )
    near = [xor(z5, "seq", 8, "back_y"), xor(z6, "seq", 16, "back_y"), xor(z6, "seq", 24, "back_y")]
    send, local = call(1, near_body, [(S, BF), (S, F32)], [where] + near + [ups, abf, fin, x4])
    got = xor(send, "seq", 6, "back_half")

    at = [attn] + [xor(attn, "seq", m, "attn") for m in (1, 2, 3)]
    even, odd = call(3, project_body, [((2048, 128), BF)] * 2, [where] + at + weight, [pltpu.VMEM((8, 512, 128), BF)], after=[send])
    swapped = xor(odd, "head", 1, "out_core")
    sums = call(1, sum_pair_body, [(T, F32), (T, BF), (T, BF), (T, BF)], [even, swapped])
    rx = [xor(sums[n], "head", 2 * n, "out_x") for n in (1, 2, 3)]
    dq, dv_part, gmap = call(
        200, grad_body,
        [((4,) + S, BF), (T, F32), (T, F32)],
        [where, do, held, far_states, kept, later],
        after=[got],
    )
    dv = call(1, value_body, [((4,) + S, BF)], [where, got, local, other, dv_part, gmap])[0]
    parts = call(
        1, sum_last_body, [((384, 128), BF)] * 4, [where, sums[0]] + rx + [dq, dv], [pltpu.VMEM((4,) + S, BF)]
    )
    home = [parts[0]] + [xor(parts[m], "seq", m, "home") for m in (1, 2, 3)]
    return tuple(call(1, place_body, [((128, 512), BF)] * 3, [where] + home))


def solution(mesh):
    in_specs = (
        P("seq", "head"),
        P("seq", "head"),
        P("seq", "head"),
        P("head", "seq"),
        P("head", "seq"),
        P(None, "head", "seq"),
        P("seq"),
        P("head", "seq"),
        P("seq", "head"),
        P("head", None, None),
    )
    out_specs = (P("seq", "head"), P("seq", "head"), P("seq", "head"))
    return jax.shard_map(shards, mesh=mesh, in_specs=in_specs, out_specs=out_specs, check_vma=False)
```
